128 devices in a mesh: img: 8 (over z, core), tile: 16 (over x, y).
Axes of the slice: x: 4, y: 4, z: 4, core: 2. Of those that a mesh axis runs over, the one named last changes fastest.
Arguments:
- features: bfloat16 [256, 2400, 256], P(('img', 'tile')), may hold values from -6 to 6
- cluster_ids: int32 [256, 4, 2400], P(('img', 'tile')), may hold values from 0 to 63
- soft_weights: bfloat16 [256, 4, 2400], P(('img', 'tile')), may hold values from 0.019897461 to 1
- counts: int32 [256], P(('img', 'tile')), may hold values from 600 to 2400, as said below
- centroids: bfloat16 [64, 256], replicated, may hold values from -3 to 3
- covariance: float32 [16384, 16384], P('img', 'tile'), may hold values from -1.5 to 1.5
Outputs:
- updated: float32 [16384, 16384], P('img', 'tile')
The draws below stay inside these ranges and needn't reach their ends.
Inputs may be any that keep to these rules, and one draw needn't show every extreme that they name: `counts`: some image has exactly 2400 valid features and some exactly 600.
All inputs are finite; a program needn't handle non-finite values.
Results may differ from the reference program's by a relative error of at most 0.0003.
Values sent between devices are 32-bit elements; how exact they have to be, the bound alone decides.
A program may use at most 64 MiB of HBM per device.

```python
import math
import jax
import jax.numpy as jnp
from jax import lax

CLUSTERS = 64
DESC = 256
TOPK = 4
MAXF = 2400
FMIN = 600
IMAGES = 256
VLAD_DIM = 16384


def draw_counts(key, part):
    first_key, second_key, third_key = jax.random.split(key, 3)
    values = jax.random.randint(first_key, (IMAGES,), FMIN, MAXF + 1, dtype=jnp.int32)
    top_at = jax.random.randint(second_key, (), 0, IMAGES, dtype=jnp.int32)
    low_at = (top_at + 1 + jax.random.randint(third_key, (), 0, IMAGES - 1, dtype=jnp.int32)) % IMAGES
    values = values.at[top_at].set(MAXF)
    values = values.at[low_at].set(FMIN)
    return values


def place_ends(result, stream_key, smallest, largest):
    longest = result.shape.index(max(result.shape))
    spots = []
    for shift in (0, 1):
        where = [jax.random.randint(jax.random.fold_in(stream_key, axis), (), 0, length) for axis, length in enumerate(result.shape)]
        where[longest] = (where[longest] + shift) % result.shape[longest]
        spots.append(tuple(where))
    return result.at[spots[0]].set(smallest).at[spots[1]].set(largest)


def block_levels(own_key, shape, shards, smallest, top_value):
    factor_of, own = 1.0, jax.random.fold_in(own_key, 6)
    for dim, parts in shards:
        heights = jnp.exp(jax.random.uniform(jax.random.fold_in(own, dim), (parts,), jnp.float32, smallest / len(shards), top_value / len(shards)))
        factor_of = factor_of * jnp.repeat(heights, shape[dim] // parts).reshape([-1 if axis == dim else 1 for axis in range(len(shape))])
    return factor_of


def normal_values(stream_key, extent, scale, limit, cuts=(), kind=jnp.bfloat16):
    level = block_levels(stream_key, extent, cuts, -0.22, 0.18) if cuts else 1.0
    entries = jax.random.normal(stream_key, extent, jnp.float32) * scale * level
    return jnp.minimum(jnp.maximum(entries, -limit), limit).astype(kind)


def setup_inputs(seed: int = 0) -> dict:
    keys = jax.random.split(jax.random.key(seed), 7)
    features = normal_values(keys[0], (IMAGES, MAXF, DESC), 1.0, 6.0, ((0, 128),))
    cluster_ids = place_ends(jax.random.randint(keys[1], (IMAGES, TOPK, MAXF), 0, CLUSTERS), jax.random.fold_in(keys[1], 1), 0, CLUSTERS - 1).astype(jnp.int32)
    soft_weights = jnp.clip(jnp.exp(math.log(1.0) - 3.9171631 * jax.random.uniform(keys[2], (IMAGES, TOPK, MAXF), jnp.float32) ** block_levels(keys[2], (IMAGES, TOPK, MAXF), ((0, 128),), -0.2, 0.2)), 0.019897461, 1.0).astype(jnp.bfloat16)
    counts = draw_counts(jax.random.fold_in(keys[6], 71), 0)
    centroids = normal_values(keys[4], (CLUSTERS, DESC), 0.5, 3.0)
    covariance = normal_values(keys[5], (VLAD_DIM, VLAD_DIM), 0.1, 1.5, ((0, 8), (1, 16)), jnp.float32)
    return {"features": features, "cluster_ids": cluster_ids, "soft_weights": soft_weights, "counts": counts, "centroids": centroids, "covariance": covariance}


def aggregate(feature_rows, id_rows, weight_rows, feature_count, centroids):
    position = jnp.arange(MAXF)
    in_range = position < feature_count
    labels = jnp.arange(CLUSTERS)
    assign = jnp.zeros((CLUSTERS, MAXF), jnp.float32)
    for slot in range(TOPK):
        matched = id_rows[slot][None, :] == labels[:, None]
        assign = assign + jnp.where(matched, weight_rows[slot].astype(jnp.float32)[None, :], jnp.float32(0.0))
    assign = jnp.where(in_range[None, :], assign, jnp.float32(0.0)).astype(jnp.bfloat16)
    weight_sum = lax.optimization_barrier(jnp.sum(assign.astype(jnp.float32), axis=1))
    residual = jnp.dot(assign, feature_rows, preferred_element_type=jnp.float32)
    residual = residual - weight_sum[:, None] * centroids.astype(jnp.float32)
    magnitude = jnp.sqrt(lax.optimization_barrier(jnp.sum(residual * residual, axis=1, keepdims=True)) + 1e-06)
    return (residual / magnitude).reshape(-1)

def reference(features, cluster_ids, soft_weights, counts, centroids, covariance):

    def one_image(packed):
        return aggregate(packed[0], packed[1], packed[2], packed[3], centroids)
    vlad_rows = lax.map(one_image, (features, cluster_ids, soft_weights, counts))
    outer_sum = jnp.dot(vlad_rows.T, vlad_rows, precision=lax.Precision.HIGHEST)
    factor = float(DESC) / float(IMAGES)
    return covariance + factor * outer_sum
```

```python
import functools

import jax
import jax.numpy as jnp
from jax import lax
from jax.experimental import pallas as pl
from jax.experimental.pallas import tpu as pltpu
from jax.sharding import PartitionSpec as P

MESH = pl.DeviceIdType.MESH
CLUSTERS, DESC, TOPK, IMAGES = 64, 256, 4, 256
SIDE = 4
ROWS = 8
COLS = 4
LANES = 128


def vlad_kernel(counts, features, ids, weights, centroids, rows):
    image = pl.program_id(0)
    slots = ids.shape[2]
    labels = lax.broadcasted_iota(jnp.int32, (CLUSTERS, 1), 0)
    in_range = lax.broadcasted_iota(jnp.int32, (1, slots), 1) < counts[image]
    assign = jnp.zeros((CLUSTERS, slots), jnp.float32)
    for slot in range(TOPK):
        weight = jnp.where(in_range, weights[0, slot : slot + 1, :].astype(jnp.float32), 0.0)
        assign = assign + jnp.where(ids[0, slot : slot + 1, :] == labels, weight, 0.0)
    assign = assign.astype(jnp.bfloat16)
    weight_sum = jnp.sum(assign.astype(jnp.float32), axis=1, keepdims=True)
    residual = jnp.dot(assign, features[0], preferred_element_type=jnp.float32)
    residual = residual - weight_sum * centroids[...].astype(jnp.float32)
    magnitude = jnp.sqrt(jnp.sum(residual * residual, axis=1, keepdims=True) + 1e-06)
    residual = residual / magnitude
    for block in range(CLUSTERS // ROWS):
        for half in range(DESC // LANES):
            rows[0, block, half] = residual[
                block * ROWS : (block + 1) * ROWS, half * LANES : (half + 1) * LANES
            ]


def gather_kernel(vlad, left, right, cols, send_sem, recv_sem, own_sem):
    img, tile = lax.axis_index("img"), lax.axis_index("tile")
    z, core, x, y = img // 2, img % 2, tile // SIDE, tile % SIDE

    def at(dx, dy, dz, dc):
        return (
            lax.rem(z + dz + SIDE, SIDE) * 2 + lax.rem(core + dc, 2),
            lax.rem(x + dx + SIDE, SIDE) * SIDE + lax.rem(y + dy + SIDE, SIDE),
        )

    column = [(0, 0, dz, dc) for dz in range(SIDE) for dc in range(2) if dz or dc]
    plane = [(dx, dy, 0, 0) for dx in range(SIDE) for dy in range(SIDE) if dx or dy]
    barrier = pltpu.get_barrier_semaphore()
    for step in column + plane:
        pl.semaphore_signal(barrier, inc=1, device_id=at(*step), device_id_type=MESH)

    for block in range(CLUSTERS // COLS):
        for k in range(2):
            for half in range(DESC // LANES):
                start = k * ROWS + half * COLS
                first_row = block * COLS % ROWS
                cols[block, start : start + COLS] = vlad[
                    k, block * COLS // ROWS, half, first_row : first_row + COLS
                ]
    pl.semaphore_wait(barrier, len(column + plane))

    copies = []

    def put(source, target, step):
        index = len(copies)
        copy = pltpu.make_async_remote_copy(
            src_ref=source,
            dst_ref=target,
            send_sem=send_sem.at[index],
            recv_sem=recv_sem.at[index],
            device_id=at(*step),
            device_id_type=MESH,
        )
        copy.start()
        copies.append(copy)
        return copy

    def block_of(index):
        return vlad.at[:, index]

    own_left = pltpu.make_async_copy(block_of(img), left.at[tile, img], own_sem.at[0])
    own_left.start()
    own_right = pltpu.make_async_copy(cols.at[tile], right.at[tile, img], own_sem.at[1])
    own_right.start()
    blocks = [put(block_of(at(*step)[0]), left.at[tile, img], step) for step in column]
    parts = [put(cols.at[at(*step)[1]], right.at[tile, img], step) for step in plane]
    own_left.wait()
    for copy in blocks:
        copy.wait_recv()

    forward, backward = ((1, 0), (0, 1)), ((-1, 0), (0, -1))

    def part(dx, dy, start, size):
        index = at(dx, dy, 0, 0)[1]
        return left.at[index, pl.ds(start, size)]

    def send(half, dx, dy, start, size, axis, sign):
        step = [0, 0, 0, 0]
        step[axis] = sign
        ref = part(dx, dy, start, size)
        return put(ref, ref, step)

    first = {}
    for half in (0, 1):
        for sign in (1, -1):
            first[half, sign] = send(half, 0, 0, 4 * half, 4, half, sign)
    second = {}
    for half in (0, 1):
        for sign in (1, -1):
            second[half, 0, sign] = send(half, 0, 0, 4 * half, 4, 1 - half, sign)

    def along(half, distance, across):
        return (distance, across) if half == 0 else (across, distance)

    relay = {}
    for half in (0, 1):
        for sign in (1, -1):
            first[half, sign].wait_recv()
            start = 4 * half + (0 if sign == 1 else 2)
            dx, dy = along(half, -sign, 0)
            relay[half, sign] = send(half, dx, dy, start, 2, half, sign)

    own_right.wait()
    for copy in parts:
        copy.wait_recv()

    def slab(dz):
        return right.at[:, at(0, 0, dz, 0)[0]]

    def half_slab(dz, top):
        return right.at[pl.ds(8 * top, 8), at(0, 0, dz, 0)[0]]

    up = put(slab(0), slab(0), (0, 0, 1, 0))
    down = put(slab(0), slab(0), (0, 0, -1, 0))
    twins = [put(slab(0), slab(0), (0, 0, 0, 1))]

    for half in (0, 1):
        for sign in (1, -1):
            dx, dy = along(half, -sign, 0)
            for turn in (1, -1):
                second[half, -sign, turn] = send(half, dx, dy, 4 * half, 4, 1 - half, turn)

    late = {}

    def hop(half, distance):
        for turn in (1, -1):
            second[half, distance, turn].wait_recv()
            dx, dy = along(half, distance, -turn)
            start = 4 * half + (0 if turn == 1 else 2)
            late[half, distance, turn] = send(half, dx, dy, start, 2, 1 - half, turn)

    for half in (0, 1):
        hop(half, 0)
    for half in (0, 1):
        for sign in (1, -1):
            relay[half, sign].wait_recv()
        dx, dy = along(half, 2, 0)
        for turn in (1, -1):
            second[half, 2, turn] = send(half, dx, dy, 4 * half, 4, 1 - half, turn)

    up.wait_recv()
    up2 = put(half_slab(-1, 0), half_slab(-1, 0), (0, 0, 1, 0))
    twins.append(put(slab(-1), slab(-1), (0, 0, 0, 1)))
    down.wait_recv()
    down2 = put(half_slab(1, 1), half_slab(1, 1), (0, 0, -1, 0))
    twins.append(put(slab(1), slab(1), (0, 0, 0, 1)))

    for distance in (1, -1):
        for half in (0, 1):
            hop(half, distance)
    up2.wait_recv()
    down2.wait_recv()
    twins.append(put(slab(2), slab(2), (0, 0, 0, 1)))
    for half in (0, 1):
        hop(half, 2)
    for copy in twins:
        copy.wait_recv()
    for copy in late.values():
        copy.wait_recv()
    for copy in copies:
        copy.wait_send()


def product_kernel(left, right, covariance, updated, high, low):
    k = pl.program_id(0)

    def split(value):
        top = value.astype(jnp.bfloat16)
        return top, (value - top.astype(jnp.float32)).astype(jnp.bfloat16)

    def cluster(ref, index, count):
        return jnp.concatenate(
            [ref[pl.ds(half * count + index, IMAGES, stride=2 * count), :] for half in range(2)], axis=1
        )

    @pl.when(k == 0)
    def _():
        for j in range(COLS):
            top, rest = split(cluster(right, j, COLS))
            high[:, j * DESC : (j + 1) * DESC] = top
            low[:, j * DESC : (j + 1) * DESC] = rest

    top, rest = split(cluster(left, k, ROWS))
    dot = functools.partial(
        lax.dot_general, dimension_numbers=(((0,), (0,)), ((), ())), preferred_element_type=jnp.float32
    )
    updated[...] = covariance[...] + (dot(top, high[...]) + (dot(rest, high[...]) + dot(top, low[...])))


def body(features, cluster_ids, soft_weights, counts, centroids, covariance):
    images, slots, _ = features.shape
    height, width = covariance.shape
    vmem = pl.BlockSpec(memory_space=pltpu.VMEM)
    vlad = pl.pallas_call(
        vlad_kernel,
        grid=(images,),
        in_specs=[
            pl.BlockSpec(memory_space=pltpu.SMEM),
            pl.BlockSpec((1, slots, DESC), lambda i: (i, 0, 0)),
            pl.BlockSpec((1, TOPK, slots), lambda i: (i, 0, 0)),
            pl.BlockSpec((1, TOPK, slots), lambda i: (i, 0, 0)),
            pl.BlockSpec((CLUSTERS, DESC), lambda i: (0, 0)),
        ],
        out_specs=pl.BlockSpec((1, CLUSTERS // ROWS, 2, ROWS, LANES), lambda i: (i, 0, 0, 0, 0)),
        out_shape=jax.ShapeDtypeStruct((images, CLUSTERS // ROWS, 2, ROWS, LANES), jnp.float32),
        compiler_params=pltpu.CompilerParams(vmem_limit_bytes=32 * 2**20),
        name="vlad",
    )(counts, features, cluster_ids, soft_weights, centroids)
    n_copies = 7 + 15 + 8 + 4 + 12 + 16 + 4 + 4 + 4
    left, right = pl.pallas_call(
        gather_kernel,
        in_specs=[vmem],
        out_specs=[vmem, vmem],
        out_shape=[
            jax.ShapeDtypeStruct((16, 8, images, 2, ROWS, LANES), jnp.float32),
            jax.ShapeDtypeStruct((16, 8, images * 2 * COLS, LANES), jnp.float32),
        ],
        scratch_shapes=[
            pltpu.VMEM((16, images * 2 * COLS, LANES), jnp.float32),
            pltpu.SemaphoreType.DMA((n_copies,)),
            pltpu.SemaphoreType.DMA((n_copies,)),
            pltpu.SemaphoreType.DMA((2,)),
        ],
        compiler_params=pltpu.CompilerParams(
            collective_id=0, has_side_effects=True, vmem_limit_bytes=32 * 2**20
        ),
        name="gather",
    )(vlad)
    return pl.pallas_call(
        product_kernel,
        grid=(height // DESC,),
        in_specs=[vmem, vmem, pl.BlockSpec((DESC, width), lambda k: (k, 0))],
        out_specs=pl.BlockSpec((DESC, width), lambda k: (k, 0)),
        out_shape=jax.ShapeDtypeStruct((height, width), jnp.float32),
        scratch_shapes=[pltpu.VMEM((IMAGES, width), jnp.bfloat16)] * 2,
        compiler_params=pltpu.CompilerParams(vmem_limit_bytes=32 * 2**20),
        name="product",
    )(left.reshape(-1, LANES), right.reshape(-1, LANES), covariance)


def solution(mesh):
    return jax.shard_map(
        body,
        mesh=mesh,
        in_specs=(
            P(("img", "tile"), None, None),
            P(("img", "tile"), None, None),
            P(("img", "tile"), None, None),
            P(("img", "tile")),
            P(),
            P("img", "tile"),
        ),
        out_specs=P("img", "tile"),
        check_vma=False,
    )
```

```python
import jax
import jax.numpy as jnp
from jax import lax
from jax.experimental import pallas as pl
from jax.experimental.pallas import tpu as pltpu
from jax.sharding import PartitionSpec as P

MESH = pl.DeviceIdType.MESH
CLUSTERS, DESC, TOPK, IMAGES = 64, 256, 4, 256
SIDE = 4
ROWS = 8
COLS = 4
LANES = 128
PLACE = {0: 0, -1: 1, 1: 2, 2: 3}
BACK = {0: 0, -1: 1, 1: -1, 2: 2}
GROUPS = {0: (0, 8), 1: (8, 16), 2: (24, 8)}


def gather_kernel(
    counts, features, ids, weights, centroids, covariance,
    left, right, total,
    count_s, feature_v, id_v, weight_v, centroid_v, vlad, cols,
    load_sem, cov_sem, own_sem,
    first_send, first_recv, next_send, next_recv, relay_send, relay_recv, col_send, col_recv,
):
    img, tile = lax.axis_index("img"), lax.axis_index("tile")
    z, core, x, y = img // 2, img % 2, tile // SIDE, tile % SIDE

    def at(dx, dy, dz, dc):
        return (
            lax.rem(z + dz + SIDE, SIDE) * 2 + lax.rem(core + dc, 2),
            lax.rem(x + dx + SIDE, SIDE) * SIDE + lax.rem(y + dy + SIDE, SIDE),
        )

    loads = [[], []]
    loads[0].append(pltpu.make_async_copy(counts, count_s, load_sem.at[0]))
    loads[0].append(pltpu.make_async_copy(centroids, centroid_v, load_sem.at[1]))
    for k in range(2):
        for n, (source, target) in enumerate(((ids, id_v), (weights, weight_v), (features, feature_v))):
            loads[k].append(pltpu.make_async_copy(source.at[k], target.at[k], load_sem.at[2 + 3 * k + n]))
    for copy in loads[0] + loads[1]:
        copy.start()

    distances = (2, 1, -1, 0)
    plane = [(dx, dy, 0, 0) for dx in distances for dy in distances if dx or dy]
    peers = list(plane)
    for d in distances:
        for dz in distances:
            for dc in range(2):
                if dz or dc:
                    peers += [(d, 0, dz, dc)] + ([(0, d, dz, dc)] if d else [])
    barrier = pltpu.get_barrier_semaphore()
    for step in peers:
        pl.semaphore_signal(barrier, inc=1, device_id=at(*step), device_id_type=MESH)
    fill = pltpu.make_async_copy(covariance, total, cov_sem.at[0])
    fill.start()

    def aggregate(k):
        for copy in loads[k]:
            copy.wait()
        slots = id_v.shape[2]
        labels = lax.broadcasted_iota(jnp.int32, (CLUSTERS, 1), 0)
        in_range = lax.broadcasted_iota(jnp.int32, (1, slots), 1) < count_s[k]
        assign = jnp.zeros((CLUSTERS, slots), jnp.float32)
        for slot in range(TOPK):
            weight = jnp.where(in_range, weight_v[k, slot : slot + 1, :].astype(jnp.float32), 0.0)
            assign = assign + jnp.where(id_v[k, slot : slot + 1, :] == labels, weight, 0.0)
        assign = assign.astype(jnp.bfloat16)
        weight_sum = jnp.sum(assign.astype(jnp.float32), axis=1, keepdims=True)
        residual = jnp.dot(assign, feature_v[k], preferred_element_type=jnp.float32)
        residual = residual - weight_sum * centroid_v[...].astype(jnp.float32)
        magnitude = jnp.sqrt(jnp.sum(residual * residual, axis=1, keepdims=True) + 1e-06)
        residual = residual / magnitude
        for half in range(2):
            lanes = slice(half * LANES, (half + 1) * LANES)
            for block in range(CLUSTERS // ROWS):
                vlad[k, block, half] = residual[block * ROWS : (block + 1) * ROWS, lanes]
            for block in range(CLUSTERS // COLS):
                start = k * 2 * COLS + half * COLS
                cols[block, start : start + COLS] = residual[block * COLS : (block + 1) * COLS, lanes]

    sent = []

    def put(source, target, send_sem, recv_sem, step):
        copy = pltpu.make_async_remote_copy(
            src_ref=source, dst_ref=target, send_sem=send_sem, recv_sem=recv_sem,
            device_id=at(*step), device_id_type=MESH,
        )
        copy.start()
        return copy

    def group_of(distance):
        return abs(distance)

    def along(k, first, second):
        return (first, second, 0, 0) if k == 0 else (second, first, 0, 0)

    def exchange(k):
        own = pltpu.make_async_copy(vlad.at[k, img], left.at[k, 0, 0], own_sem.at[k])
        own.start()
        for d in (0, 2, 1, -1):
            for dz in (2, 1, -1, 0):
                for dc in range(2):
                    if d or dz or dc:
                        step = along(k, d, 0)[:2] + (dz, dc)
                        slot = PLACE[BACK[d]] * 8 + PLACE[BACK[dz]] * 2 + dc
                        put(
                            vlad.at[k, at(*step)[0]], left.at[k, 0, slot],
                            first_send.at[k], first_recv.at[k, group_of(d)], step,
                        )
        return own

    def arrived(ref, sem):
        pltpu.make_async_copy(ref, ref, sem).wait()

    aggregate(0)
    pl.semaphore_wait(barrier, len(peers))
    own = [exchange(0)]
    aggregate(1)
    own.append(exchange(1))
    own_cols = pltpu.make_async_copy(cols.at[tile], right.at[0, 0], own_sem.at[2])
    own_cols.start()
    for step in plane:
        slot = PLACE[BACK[step[0]]] * SIDE + PLACE[BACK[step[1]]]
        put(cols.at[at(*step)[1]], right.at[slot, 0], col_send.at[0], col_recv.at[0], step)

    onward = {}

    def second(k, group):
        start, size = GROUPS[group]
        if group == 0:
            own[k].wait()
            arrived(left.at[k, 0, pl.ds(1, 7)], first_recv.at[k, 0])
        else:
            arrived(left.at[k, 0, pl.ds(start, size)], first_recv.at[k, group])
        slots = pl.ds(start, size)
        for n, turn in enumerate((1, -1)):
            onward[k, group, turn] = put(
                left.at[k, 0, slots], left.at[k, PLACE[-turn], slots],
                next_send.at[k, group, n], next_recv.at[k, group, n], along(k, 0, turn),
            )
            sent.append(onward[k, group, turn])

    relays = []

    def relay(k, group):
        start, size = GROUPS[group]
        for n, turn in enumerate((1, -1)):
            onward[k, group, turn].wait_recv()
            slots = pl.ds(start + n * size // 2, size // 2)
            relays.append(
                put(
                    left.at[k, PLACE[-turn], slots], left.at[k, PLACE[2], slots],
                    relay_send.at[k, group, n], relay_recv.at[k, group, n], along(k, 0, turn),
                )
            )

    second(0, 0)
    second(1, 0)
    second(0, 1)
    second(1, 1)
    own_cols.wait()
    arrived(right.at[pl.ds(1, 15), 0], col_recv.at[0])

    def slab(dz, dc):
        return right.at[:, PLACE[dz] * 2 + dc]

    def twin(dz):
        n = 4 + PLACE[dz]
        return put(slab(dz, 0), slab(dz, 1), col_send.at[n], col_recv.at[n], (0, 0, 0, 1))

    spread = [
        put(slab(0, 0), slab(BACK[dz], 0), col_send.at[PLACE[dz]], col_recv.at[PLACE[dz]], (0, 0, dz, 0))
        for dz in (2, 1, -1)
    ]
    twins = [twin(0)]
    second(0, 2)
    second(1, 2)
    relay(0, 0)
    relay(1, 0)
    for copy, dz in zip(spread, (2, -1, 1)):
        copy.wait_recv()
        twins.append(twin(dz))
    relay(0, 1)
    relay(1, 1)
    for k in range(2):
        arrived(left.at[k, 0, pl.ds(1, 31)], first_send.at[k])
    arrived(cols.at[pl.ds(1, 15)], col_send.at[0])
    relay(0, 2)
    relay(1, 2)
    fill.wait()
    for copy in twins:
        copy.wait_recv()
    for copy in spread + twins + sent:
        copy.wait_send()
    for copy in relays:
        copy.wait()


def product_kernel(left, right, total, updated, factor):
    k = pl.program_id(0)

    def split(value):
        top = value.astype(jnp.bfloat16)
        return top, (value - top.astype(jnp.float32)).astype(jnp.bfloat16)

    @pl.when(k == 0)
    def _():
        for j in range(COLS):
            pieces = []
            for image in range(2):
                for second in range(SIDE):
                    for first in range(SIDE):
                        dx, dy = (first, second) if image == 0 else (second, first)
                        base = (dx * SIDE + dy) * 8 * 16 + image * 8 + j
                        pieces.append(
                            jnp.concatenate(
                                [right[pl.ds(base + 4 * half, 8, stride=16), :] for half in range(2)], axis=1
                            )
                        )
            top, rest = split(jnp.concatenate(pieces, axis=0))
            columns = slice(j * DESC, (j + 1) * DESC)
            factor[:IMAGES, columns] = top
            factor[IMAGES : 2 * IMAGES, columns] = top
            factor[2 * IMAGES :, columns] = rest

    top, rest = split(
        jnp.concatenate([left[pl.ds(half * ROWS + k, IMAGES, stride=2 * ROWS), :] for half in range(2)], axis=1)
    )
    updated[...] = total[pl.ds(pl.multiple_of(k * DESC, DESC), DESC), :] + lax.dot_general(
        jnp.concatenate([top, rest, top], axis=0),
        factor[...],
        (((0,), (0,)), ((), ())),
        preferred_element_type=jnp.float32,
    )


def body(features, cluster_ids, soft_weights, counts, centroids, covariance):
    images, slots, _ = features.shape
    height, width = covariance.shape
    vmem = pl.BlockSpec(memory_space=pltpu.VMEM)
    hbm = pl.BlockSpec(memory_space=pltpu.HBM)
    dma = pltpu.SemaphoreType.DMA
    left, right, total = pl.pallas_call(
        gather_kernel,
        in_specs=[hbm] * 6,
        out_specs=[vmem] * 3,
        out_shape=[
            jax.ShapeDtypeStruct((images, SIDE, 32, 2, ROWS, LANES), jnp.float32),
            jax.ShapeDtypeStruct((16, 8, images * 2 * COLS, LANES), jnp.float32),
            jax.ShapeDtypeStruct((height, width), jnp.float32),
        ],
        scratch_shapes=[
            pltpu.SMEM((images,), jnp.int32),
            pltpu.VMEM(features.shape, features.dtype),
            pltpu.VMEM(cluster_ids.shape, cluster_ids.dtype),
            pltpu.VMEM(soft_weights.shape, soft_weights.dtype),
            pltpu.VMEM(centroids.shape, centroids.dtype),
            pltpu.VMEM((images, CLUSTERS // ROWS, 2, ROWS, LANES), jnp.float32),
            pltpu.VMEM((16, images * 2 * COLS, LANES), jnp.float32),
            dma((8,)), dma((1,)), dma((3,)),
            dma((2,)), dma((2, 3)), dma((2, 3, 2)), dma((2, 3, 2)), dma((2, 3, 2)), dma((2, 3, 2)),
            dma((8,)), dma((8,)),
        ],
        compiler_params=pltpu.CompilerParams(
            collective_id=0, has_side_effects=True, vmem_limit_bytes=32 * 2**20
        ),
        name="gather",
    )(*(
        pltpu.with_memory_space_constraint(value, pltpu.HBM)
        for value in (counts, features, cluster_ids, soft_weights, centroids, covariance)
    ))
    return pl.pallas_call(
        product_kernel,
        grid=(height // DESC,),
        in_specs=[vmem] * 3,
        out_specs=pl.BlockSpec((DESC, width), lambda k: (k, 0)),
        out_shape=jax.ShapeDtypeStruct((height, width), jnp.float32),
        scratch_shapes=[pltpu.VMEM((3 * IMAGES, width), jnp.bfloat16)],
        compiler_params=pltpu.CompilerParams(vmem_limit_bytes=32 * 2**20),
        name="product",
    )(left.reshape(-1, LANES), right.reshape(-1, LANES), total)


def solution(mesh):
    return jax.shard_map(
        body,
        mesh=mesh,
        in_specs=(
            P(("img", "tile"), None, None),
            P(("img", "tile"), None, None),
            P(("img", "tile"), None, None),
            P(("img", "tile")),
            P(),
            P("img", "tile"),
        ),
        out_specs=P("img", "tile"),
        check_vma=False,
    )
```

```python
import jax
import jax.numpy as jnp
from jax import lax
from jax.experimental import pallas as pl
from jax.experimental.pallas import tpu as pltpu
from jax.sharding import PartitionSpec as P

MESH = pl.DeviceIdType.MESH
CLUSTERS, DESC, TOPK, IMAGES = 64, 256, 4, 256
SIDE = 4
ROWS = 8
COLS = 4
LANES = 128
PLACE = {0: 0, -1: 1, 1: 2, 2: 3}
BACK = {0: 0, -1: 1, 1: -1, 2: 2}
DIMS = (((0,), (0,)), ((), ()))


def split(value):
    top = value.astype(jnp.bfloat16)
    return top, (value - top.astype(jnp.float32)).astype(jnp.bfloat16)


def columns_of(right, v):
    blocks = []
    for j in range(COLS):
        halves = []
        for half in range(2):
            halves.append(
                jnp.concatenate(
                    [
                        right[pl.ds((zc * SIDE + v) * 64 + half * COLS + j, 8, stride=8), :]
                        for zc in range(8)
                    ],
                    axis=0,
                )
            )
        blocks.append(jnp.concatenate(halves, axis=1))
    top, rest = split(jnp.concatenate(blocks, axis=1))
    return top, rest


def rows_of(left, start, count, k):
    top, rest = split(
        jnp.concatenate(
            [left[pl.ds(start * 16 + half * ROWS + k, count, stride=16), :] for half in range(2)], axis=1
        )
    )
    return jnp.concatenate([top, rest, top], axis=0)


def gather_kernel(
    counts, features, ids, weights, centroids, covariance,
    left, right, total,
    count_s, feature_v, id_v, weight_v, centroid_v, vlad, cols, factor,
    load_sem, cov_sem, z_send, z_recv, u_send, u_recv, v_send, v_recv, r_send, r_recv,
    c_send, c_recv, s_send, s_recv,
):
    img, tile = lax.axis_index("img"), lax.axis_index("tile")
    z, core, x, y = img // 2, img % 2, tile // SIDE, tile % SIDE

    def at(dx, dy, dz, dc):
        return (
            lax.rem(z + dz + SIDE, SIDE) * 2 + lax.rem(core + dc, 2),
            lax.rem(x + dx + SIDE, SIDE) * SIDE + lax.rem(y + dy + SIDE, SIDE),
        )

    loads = [[], []]
    loads[0].append(pltpu.make_async_copy(counts, count_s, load_sem.at[0]))
    loads[0].append(pltpu.make_async_copy(centroids, centroid_v, load_sem.at[1]))
    for k in range(2):
        for n, (source, target) in enumerate(((ids, id_v), (weights, weight_v), (features, feature_v))):
            loads[k].append(pltpu.make_async_copy(source.at[k], target.at[k], load_sem.at[2 + 3 * k + n]))
    for copy in loads[0] + loads[1]:
        copy.start()

    distances = (2, 1, -1, 0)
    plane = [(dx, dy, 0, 0) for dx in distances for dy in distances if dx or dy]
    column = [(0, 0, dz, dc) for dz in distances for dc in (1, 0) if dz or dc]
    barrier = pltpu.get_barrier_semaphore()
    for step in plane + column:
        pl.semaphore_signal(barrier, inc=1, device_id=at(*step), device_id_type=MESH)
    fill = pltpu.make_async_copy(covariance, total, cov_sem.at[0])
    fill.start()

    def aggregate(k):
        for copy in loads[k]:
            copy.wait()
        slots = id_v.shape[2]
        labels = lax.broadcasted_iota(jnp.int32, (CLUSTERS, 1), 0)
        in_range = lax.broadcasted_iota(jnp.int32, (1, slots), 1) < count_s[k]
        assign = jnp.zeros((CLUSTERS, slots), jnp.float32)
        for slot in range(TOPK):
            weight = jnp.where(in_range, weight_v[k, slot : slot + 1, :].astype(jnp.float32), 0.0)
            assign = assign + jnp.where(id_v[k, slot : slot + 1, :] == labels, weight, 0.0)
        assign = assign.astype(jnp.bfloat16)
        weight_sum = jnp.sum(assign.astype(jnp.float32), axis=1, keepdims=True)
        residual = jnp.dot(assign, feature_v[k], preferred_element_type=jnp.float32)
        residual = residual - weight_sum * centroid_v[...].astype(jnp.float32)
        magnitude = jnp.sqrt(jnp.sum(residual * residual, axis=1, keepdims=True) + 1e-06)
        residual = residual / magnitude
        for half in range(2):
            lanes = slice(half * LANES, (half + 1) * LANES)
            for block in range(CLUSTERS // ROWS):
                vlad[k, block, half] = residual[block * ROWS : (block + 1) * ROWS, lanes]
            for block in range(CLUSTERS // COLS):
                cols[block, k, half * COLS : (half + 1) * COLS] = residual[block * COLS : (block + 1) * COLS, lanes]

    def put(source, target, send_sem, recv_sem, step):
        copy = pltpu.make_async_remote_copy(
            src_ref=source, dst_ref=target, send_sem=send_sem, recv_sem=recv_sem,
            device_id=at(*step), device_id_type=MESH,
        )
        copy.start()
        return copy

    def wait(ref, sem):
        pltpu.make_async_copy(ref, ref, sem).wait()

    def along(k, u, v):
        return (u, v, 0, 0) if k == 0 else (v, u, 0, 0)

    def column_pieces(k):
        pltpu.make_async_copy(cols.at[tile, k], right.at[0, 0, 0, k, 0], c_recv.at[0]).start()
        for step in plane:
            u, v = step[:2] if k == 0 else (step[1], step[0])
            target = right.at[0, 0, PLACE[BACK[v]], k, PLACE[BACK[u]]]
            put(cols.at[at(*step)[1], k], target, c_send.at[0], c_recv.at[0], step)

    def row_pieces(k):
        pltpu.make_async_copy(vlad.at[k, img], left.at[0, 0, 0, k, 0], z_recv.at[k, 0]).start()
        for step in column:
            n = PLACE[BACK[step[2]]]
            put(vlad.at[k, at(*step)[0]], left.at[0, n, step[3], k, 0], z_send.at[k], z_recv.at[k, n], step)

    def go_u(k, j):
        wait(left.at[0, j, :, k, 0], z_recv.at[k, j])
        for u in (2, 1, -1):
            target = left.at[0, j, :, k, PLACE[BACK[u]]]
            put(left.at[0, j, :, k, 0], target, u_send.at[k], u_recv.at[k, j], along(k, u, 0))

    onward = {}

    def go_v(k, j):
        wait(left.at[0, j, :, k, pl.ds(1, 3)], u_recv.at[k, j])
        for n, turn in enumerate((1, -1)):
            target = left.at[PLACE[-turn], j, :, k]
            onward[k, j, n] = put(
                left.at[0, j, :, k], target, v_send.at[k], v_recv.at[k, j, n], along(k, 0, turn)
            )

    def relay(k, j):
        for n, turn in enumerate((1, -1)):
            onward[k, j, n].wait_recv()
            source = left.at[PLACE[-turn], j, :, k, pl.ds(2 * n, 2)]
            target = left.at[PLACE[2], j, :, k, pl.ds(2 * n, 2)]
            put(source, target, r_send.at[k], r_recv.at[k], along(k, 0, turn))

    def twin(dz):
        n = PLACE[dz]
        return put(right.at[n, 0], right.at[n, 1], s_send.at[n + 4], s_recv.at[n + 4], (0, 0, 0, 1))

    aggregate(0)
    pl.semaphore_wait(barrier, len(plane + column))
    column_pieces(0)
    row_pieces(0)
    aggregate(1)
    column_pieces(1)
    row_pieces(1)
    for j in range(SIDE):
        for k in range(2):
            go_u(k, j)
    wait(right.at[0, 0], c_recv.at[0])
    spread = {
        dz: put(
            right.at[0, 0], right.at[PLACE[BACK[dz]], 0], s_send.at[PLACE[dz]], s_recv.at[PLACE[dz]],
            (0, 0, dz, 0),
        )
        for dz in (2, 1, -1)
    }
    twins = [twin(0)]
    for j in range(2):
        for k in range(2):
            go_v(k, j)
    for k in range(2):
        go_v(k, 2)
    for k in range(2):
        relay(k, 0)
    for dz in (1, -1):
        spread[dz].wait_recv()
        twins.append(twin(BACK[dz]))
    for k in range(2):
        go_v(k, 3)
    for k in range(2):
        relay(k, 1)
    spread[2].wait_recv()
    twins.append(twin(2))
    for k in range(2):
        relay(k, 2)
    for k in range(2):
        relay(k, 3)
    for copy in twins:
        copy.wait_recv()

    flat_right = right.reshape(-1, LANES)
    flat_left = left.reshape(-1, LANES)
    for v in range(SIDE - 1):
        top, rest = columns_of(flat_right, v)
        factor[v * 64 : (v + 1) * 64] = top
        factor[192 + v * 64 : 192 + (v + 1) * 64] = top
        factor[384 + v * 64 : 384 + (v + 1) * 64] = rest
    fill.wait()
    for k in range(ROWS):
        total[k * DESC : (k + 1) * DESC] += lax.dot_general(
            rows_of(flat_left, 0, 192, k), factor[...], DIMS, preferred_element_type=jnp.float32
        )

    wait(cols.at[pl.ds(0, 15)], c_send.at[0])
    for copy in list(spread.values()) + twins:
        copy.wait_send()
    for k in range(2):
        wait(vlad.at[k, pl.ds(0, 7)], z_send.at[k])
        wait(left.at[0, :, :, k, pl.ds(1, 3)], u_send.at[k])
        wait(left.at[pl.ds(1, 2), :, :, k], v_send.at[k])
        wait(left.at[3, :, :, k], r_send.at[k])
        wait(left.at[3, :, :, k], r_recv.at[k])


def product_kernel(left, right, total, updated, staged, factor, sems):
    top, rest = columns_of(right, SIDE - 1)
    factor[:64] = top
    factor[64:128] = top
    factor[128:] = rest
    copies = []
    for k in range(ROWS):
        rows = slice(k * DESC, (k + 1) * DESC)
        staged[rows] = total[rows] + lax.dot_general(
            rows_of(left, 192, 64, k), factor[...], DIMS, preferred_element_type=jnp.float32
        )
        copies.append(pltpu.make_async_copy(staged.at[rows], updated.at[rows], sems.at[k]))
        copies[-1].start()
    for copy in copies:
        copy.wait()


def body(features, cluster_ids, soft_weights, counts, centroids, covariance):
    images = features.shape[0]
    height, width = covariance.shape
    vmem = pl.BlockSpec(memory_space=pltpu.VMEM)
    hbm = pl.BlockSpec(memory_space=pltpu.HBM)
    dma = pltpu.SemaphoreType.DMA
    operands = (counts, features, cluster_ids, soft_weights, centroids, covariance)
    left, right, total = pl.pallas_call(
        gather_kernel,
        in_specs=[hbm] * 6,
        out_specs=[vmem] * 3,
        out_shape=[
            jax.ShapeDtypeStruct((SIDE, SIDE, 2, images, SIDE, 2, ROWS, LANES), jnp.float32),
            jax.ShapeDtypeStruct((SIDE, 2, SIDE, images, SIDE, 2 * COLS, LANES), jnp.float32),
            jax.ShapeDtypeStruct((height, width), jnp.float32),
        ],
        scratch_shapes=[
            pltpu.SMEM((images,), jnp.int32),
            pltpu.VMEM(features.shape, features.dtype),
            pltpu.VMEM(cluster_ids.shape, cluster_ids.dtype),
            pltpu.VMEM(soft_weights.shape, soft_weights.dtype),
            pltpu.VMEM(centroids.shape, centroids.dtype),
            pltpu.VMEM((images, CLUSTERS // ROWS, 2, ROWS, LANES), jnp.float32),
            pltpu.VMEM((16, images, 2 * COLS, LANES), jnp.float32),
            pltpu.VMEM((3 * 192, width), jnp.bfloat16),
            dma((8,)), dma((1,)), dma((2,)), dma((2, 4)), dma((2,)), dma((2, 4)),
            dma((2,)), dma((2, 4, 2)), dma((2,)), dma((2,)), dma((1,)), dma((1,)), dma((8,)), dma((8,)),
        ],
        compiler_params=pltpu.CompilerParams(
            collective_id=0, has_side_effects=True, vmem_limit_bytes=32 * 2**20
        ),
        name="gather",
    )(*(pltpu.with_memory_space_constraint(value, pltpu.HBM) for value in operands))
    return pl.pallas_call(
        product_kernel,
        in_specs=[vmem] * 3,
        out_specs=hbm,
        out_shape=jax.ShapeDtypeStruct((height, width), jnp.float32),
        scratch_shapes=[
            pltpu.VMEM((height, width), jnp.float32),
            pltpu.VMEM((192, width), jnp.bfloat16),
            dma((ROWS,)),
        ],
        compiler_params=pltpu.CompilerParams(vmem_limit_bytes=32 * 2**20),
        name="product",
    )(left.reshape(-1, LANES), right.reshape(-1, LANES), total)


def solution(mesh):
    return jax.shard_map(
        body,
        mesh=mesh,
        in_specs=(
            P(("img", "tile"), None, None),
            P(("img", "tile"), None, None),
            P(("img", "tile"), None, None),
            P(("img", "tile")),
            P(),
            P("img", "tile"),
        ),
        out_specs=P("img", "tile"),
        check_vma=False,
    )
```

```python
import jax
import jax.numpy as jnp
from jax import lax
from jax.experimental import pallas as pl
from jax.experimental.pallas import tpu as pltpu
from jax.sharding import PartitionSpec as P

MESH = pl.DeviceIdType.MESH
CLUSTERS, DESC, TOPK, IMAGES = 64, 256, 4, 256
SIDE = 4
ROWS = 8
COLS = 4
LANES = 128
PLACE = {0: 0, -1: 1, 1: 2, 2: 3}
BACK = {0: 0, -1: 1, 1: -1, 2: 2}
DIMS = (((0,), (0,)), ((), ()))


def split(value):
    top = value.astype(jnp.bfloat16)
    return top, (value - top.astype(jnp.float32)).astype(jnp.bfloat16)


def columns_of(right, v):
    blocks = []
    for j in range(COLS):
        halves = []
        for half in range(2):
            halves.append(
                jnp.concatenate(
                    [
                        right[pl.ds((zc * SIDE + v) * 64 + half * COLS + j, 8, stride=8), :]
                        for zc in range(8)
                    ],
                    axis=0,
                )
            )
        blocks.append(jnp.concatenate(halves, axis=1))
    top, rest = split(jnp.concatenate(blocks, axis=1))
    return top, rest


def rows_of(left, start, count, k):
    top, rest = split(
        jnp.concatenate(
            [left[pl.ds(start * 16 + half * ROWS + k, count, stride=16), :] for half in range(2)], axis=1
        )
    )
    return jnp.concatenate([top, rest, top], axis=0)


def gather_kernel(
    counts, features, ids, weights, centroids, covariance,
    left, right, total,
    count_s, feature_v, id_v, weight_v, centroid_v, vlad, cols, factor,
    load_sem, cov_sem, z_send, z_recv, u_send, u_recv, v_send, v_recv, r_send, r_recv,
    c_send, c_recv, s_send, s_recv,
):
    img, tile = lax.axis_index("img"), lax.axis_index("tile")
    z, core, x, y = img // 2, img % 2, tile // SIDE, tile % SIDE

    def at(dx, dy, dz, dc):
        return (
            lax.rem(z + dz + SIDE, SIDE) * 2 + lax.rem(core + dc, 2),
            lax.rem(x + dx + SIDE, SIDE) * SIDE + lax.rem(y + dy + SIDE, SIDE),
        )

    loads = [[], []]
    loads[0].append(pltpu.make_async_copy(counts, count_s, load_sem.at[0]))
    loads[0].append(pltpu.make_async_copy(centroids, centroid_v, load_sem.at[1]))
    for k in range(2):
        for n, (source, target) in enumerate(((ids, id_v), (weights, weight_v), (features, feature_v))):
            loads[k].append(pltpu.make_async_copy(source.at[k], target.at[k], load_sem.at[2 + 3 * k + n]))
    for copy in loads[0] + loads[1]:
        copy.start()

    distances = (2, 1, -1, 0)
    plane = [(dx, dy, 0, 0) for dx in distances for dy in distances if dx or dy]
    column = [(0, 0, dz, dc) for dz in distances for dc in (1, 0) if dz or dc]
    barrier = pltpu.get_barrier_semaphore()
    for step in plane + column:
        pl.semaphore_signal(barrier, inc=1, device_id=at(*step), device_id_type=MESH)
    fill = pltpu.make_async_copy(covariance, total, cov_sem.at[0])
    fill.start()

    def aggregate(k):
        for copy in loads[k]:
            copy.wait()
        slots = id_v.shape[2]
        labels = lax.broadcasted_iota(jnp.int32, (CLUSTERS, 1), 0)
        in_range = lax.broadcasted_iota(jnp.int32, (1, slots), 1) < count_s[k]
        assign = jnp.zeros((CLUSTERS, slots), jnp.float32)
        for slot in range(TOPK):
            weight = jnp.where(in_range, weight_v[k, slot : slot + 1, :].astype(jnp.float32), 0.0)
            assign = assign + jnp.where(id_v[k, slot : slot + 1, :] == labels, weight, 0.0)
        assign = assign.astype(jnp.bfloat16)
        weight_sum = jnp.sum(assign.astype(jnp.float32), axis=1, keepdims=True)
        residual = jnp.dot(assign, feature_v[k], preferred_element_type=jnp.float32)
        residual = residual - weight_sum * centroid_v[...].astype(jnp.float32)
        magnitude = jnp.sqrt(jnp.sum(residual * residual, axis=1, keepdims=True) + 1e-06)
        residual = residual / magnitude
        for half in range(2):
            lanes = slice(half * LANES, (half + 1) * LANES)
            for block in range(CLUSTERS // ROWS):
                vlad[k, block, half] = residual[block * ROWS : (block + 1) * ROWS, lanes]
            for block in range(CLUSTERS // COLS):
                cols[block, k, half * COLS : (half + 1) * COLS] = residual[block * COLS : (block + 1) * COLS, lanes]

    def put(source, target, send_sem, recv_sem, step):
        copy = pltpu.make_async_remote_copy(
            src_ref=source, dst_ref=target, send_sem=send_sem, recv_sem=recv_sem,
            device_id=at(*step), device_id_type=MESH,
        )
        copy.start()
        return copy

    def wait(ref, sem):
        pltpu.make_async_copy(ref, ref, sem).wait()

    def along(k, u, v):
        return (u, v, 0, 0) if k == 0 else (v, u, 0, 0)

    def column_pieces(k):
        pltpu.make_async_copy(cols.at[tile, k], right.at[0, 0, 0, k, 0], c_recv.at[0]).start()
        for step in plane:
            u, v = step[:2] if k == 0 else (step[1], step[0])
            target = right.at[0, 0, PLACE[BACK[v]], k, PLACE[BACK[u]]]
            put(cols.at[at(*step)[1], k], target, c_send.at[0], c_recv.at[0], step)

    def row_pieces(k):
        pltpu.make_async_copy(vlad.at[k, img], left.at[0, 0, 0, k, 0], z_recv.at[k, 0]).start()
        for step in column:
            n = PLACE[BACK[step[2]]]
            put(vlad.at[k, at(*step)[0]], left.at[0, n, step[3], k, 0], z_send.at[k], z_recv.at[k, n], step)

    def go_u(k, j):
        wait(left.at[0, j, :, k, 0], z_recv.at[k, j])
        for u in (2, 1, -1):
            target = left.at[0, j, :, k, PLACE[BACK[u]]]
            put(left.at[0, j, :, k, 0], target, u_send.at[k], u_recv.at[k, j], along(k, u, 0))

    onward = {}

    def go_v(k, j):
        wait(left.at[0, j, :, k, pl.ds(1, 3)], u_recv.at[k, j])
        for n, turn in enumerate((1, -1)):
            target = left.at[PLACE[-turn], j, :, k]
            onward[k, j, n] = put(
                left.at[0, j, :, k], target, v_send.at[k], v_recv.at[k, j, n], along(k, 0, turn)
            )

    def relay(k, j):
        for n, turn in enumerate((1, -1)):
            onward[k, j, n].wait_recv()
            source = left.at[PLACE[-turn], j, :, k, pl.ds(2 * n, 2)]
            target = left.at[PLACE[2], j, :, k, pl.ds(2 * n, 2)]
            put(source, target, r_send.at[k], r_recv.at[k], along(k, 0, turn))

    def twin(dz):
        n = PLACE[dz]
        return put(right.at[n, 0], right.at[n, 1], s_send.at[n + 4], s_recv.at[n + 4], (0, 0, 0, 1))

    aggregate(0)
    pl.semaphore_wait(barrier, len(plane + column))
    column_pieces(0)
    row_pieces(0)
    aggregate(1)
    column_pieces(1)
    row_pieces(1)
    for k in range(2):
        go_u(k, 0)
    for k in range(2):
        go_u(k, 1)
    for k in range(2):
        go_u(k, 2)
    for k in range(2):
        go_u(k, 3)
    wait(right.at[0, 0], c_recv.at[0])
    spread = {
        dz: put(
            right.at[0, 0], right.at[PLACE[BACK[dz]], 0], s_send.at[PLACE[dz]], s_recv.at[PLACE[dz]],
            (0, 0, dz, 0),
        )
        for dz in (2, 1, -1)
    }
    twins = [twin(0)]
    for k in range(2):
        go_v(k, 0)
    for k in range(2):
        go_v(k, 1)
    for k in range(2):
        go_v(k, 2)
    for k in range(2):
        go_v(k, 3)
    for dz in (1, -1):
        spread[dz].wait_recv()
        twins.append(twin(BACK[dz]))
    for k in range(2):
        relay(k, 0)
    for k in range(2):
        relay(k, 1)
    spread[2].wait_recv()
    twins.append(twin(2))
    for k in range(2):
        relay(k, 2)
    for k in range(2):
        relay(k, 3)
    for copy in twins:
        copy.wait_recv()

    flat_right = right.reshape(-1, LANES)
    flat_left = left.reshape(-1, LANES)
    for v in range(SIDE - 1):
        top, rest = columns_of(flat_right, v)
        factor[v * 64 : (v + 1) * 64] = top
        factor[192 + v * 64 : 192 + (v + 1) * 64] = top
        factor[384 + v * 64 : 384 + (v + 1) * 64] = rest
    fill.wait()
    for k in range(ROWS):
        total[k * DESC : (k + 1) * DESC] += lax.dot_general(
            rows_of(flat_left, 0, 192, k), factor[...], DIMS, preferred_element_type=jnp.float32
        )

    wait(cols.at[pl.ds(0, 15)], c_send.at[0])
    for copy in list(spread.values()) + twins:
        copy.wait_send()
    for k in range(2):
        wait(vlad.at[k, pl.ds(0, 7)], z_send.at[k])
        wait(left.at[0, :, :, k, pl.ds(1, 3)], u_send.at[k])
        wait(left.at[pl.ds(1, 2), :, :, k], v_send.at[k])
        wait(left.at[3, :, :, k], r_send.at[k])
        wait(left.at[3, :, :, k], r_recv.at[k])


def product_kernel(left, right, total, updated, staged, factor, sems):
    top, rest = columns_of(right, SIDE - 1)
    factor[:64] = top
    factor[64:128] = top
    factor[128:] = rest
    copies = []
    for k in range(ROWS):
        rows = slice(k * DESC, (k + 1) * DESC)
        staged[rows] = total[rows] + lax.dot_general(
            rows_of(left, 192, 64, k), factor[...], DIMS, preferred_element_type=jnp.float32
        )
        copies.append(pltpu.make_async_copy(staged.at[rows], updated.at[rows], sems.at[k]))
        copies[-1].start()
    for copy in copies:
        copy.wait()


def body(features, cluster_ids, soft_weights, counts, centroids, covariance):
    images = features.shape[0]
    height, width = covariance.shape
    vmem = pl.BlockSpec(memory_space=pltpu.VMEM)
    hbm = pl.BlockSpec(memory_space=pltpu.HBM)
    dma = pltpu.SemaphoreType.DMA
    operands = (counts, features, cluster_ids, soft_weights, centroids, covariance)
    left, right, total = pl.pallas_call(
        gather_kernel,
        in_specs=[hbm] * 6,
        out_specs=[vmem] * 3,
        out_shape=[
            jax.ShapeDtypeStruct((SIDE, SIDE, 2, images, SIDE, 2, ROWS, LANES), jnp.float32),
            jax.ShapeDtypeStruct((SIDE, 2, SIDE, images, SIDE, 2 * COLS, LANES), jnp.float32),
            jax.ShapeDtypeStruct((height, width), jnp.float32),
        ],
        scratch_shapes=[
            pltpu.SMEM((images,), jnp.int32),
            pltpu.VMEM(features.shape, features.dtype),
            pltpu.VMEM(cluster_ids.shape, cluster_ids.dtype),
            pltpu.VMEM(soft_weights.shape, soft_weights.dtype),
            pltpu.VMEM(centroids.shape, centroids.dtype),
            pltpu.VMEM((images, CLUSTERS // ROWS, 2, ROWS, LANES), jnp.float32),
            pltpu.VMEM((16, images, 2 * COLS, LANES), jnp.float32),
            pltpu.VMEM((3 * 192, width), jnp.bfloat16),
            dma((8,)), dma((1,)), dma((2,)), dma((2, 4)), dma((2,)), dma((2, 4)),
            dma((2,)), dma((2, 4, 2)), dma((2,)), dma((2,)), dma((1,)), dma((1,)), dma((8,)), dma((8,)),
        ],
        compiler_params=pltpu.CompilerParams(
            collective_id=0, has_side_effects=True, vmem_limit_bytes=32 * 2**20
        ),
        name="gather",
    )(*(pltpu.with_memory_space_constraint(value, pltpu.HBM) for value in operands))
    return pl.pallas_call(
        product_kernel,
        in_specs=[vmem] * 3,
        out_specs=hbm,
        out_shape=jax.ShapeDtypeStruct((height, width), jnp.float32),
        scratch_shapes=[
            pltpu.VMEM((height, width), jnp.float32),
            pltpu.VMEM((192, width), jnp.bfloat16),
            dma((ROWS,)),
        ],
        compiler_params=pltpu.CompilerParams(vmem_limit_bytes=32 * 2**20),
        name="product",
    )(left.reshape(-1, LANES), right.reshape(-1, LANES), total)


def solution(mesh):
    return jax.shard_map(
        body,
        mesh=mesh,
        in_specs=(
            P(("img", "tile"), None, None),
            P(("img", "tile"), None, None),
            P(("img", "tile"), None, None),
            P(("img", "tile")),
            P(),
            P("img", "tile"),
        ),
        out_specs=P("img", "tile"),
        check_vma=False,
    )
```

```python
import jax
import jax.numpy as jnp
from jax import lax
from jax.experimental import pallas as pl
from jax.experimental.pallas import tpu as pltpu
from jax.sharding import PartitionSpec as P

MESH = pl.DeviceIdType.MESH
CLUSTERS, DESC, TOPK, IMAGES = 64, 256, 4, 256
SIDE = 4
ROWS = 8
COLS = 4
LANES = 128
PLACE = {0: 0, -1: 1, 1: 2, 2: 3}
BACK = {0: 0, -1: 1, 1: -1, 2: 2}
DIMS = (((0,), (0,)), ((), ()))


def split(value):
    top = value.astype(jnp.bfloat16)
    return top, (value - top.astype(jnp.float32)).astype(jnp.bfloat16)


def columns_of(right, v):
    blocks = []
    for j in range(COLS):
        halves = []
        for half in range(2):
            halves.append(
                jnp.concatenate(
                    [
                        right[pl.ds((zc * SIDE + v) * 64 + half * COLS + j, 8, stride=8), :]
                        for zc in range(8)
                    ],
                    axis=0,
                )
            )
        blocks.append(jnp.concatenate(halves, axis=1))
    top, rest = split(jnp.concatenate(blocks, axis=1))
    return top, rest


def rows_of(left, start, count, k):
    top, rest = split(
        jnp.concatenate(
            [left[pl.ds(start * 16 + half * ROWS + k, count, stride=16), :] for half in range(2)], axis=1
        )
    )
    return jnp.concatenate([top, rest, top], axis=0)


def gather_kernel(
    counts, features, ids, weights, centroids, covariance,
    left, right, total, spare_rows, spare_columns,
    count_s, feature_v, id_v, weight_v, centroid_v, vlad, cols, factor, stacked,
    load_sem, cov_sem, z_send, z_recv, u_send, u_recv, v_send, v_recv, r_send, r_recv,
    c_send, c_recv, s_send, s_recv,
):
    img, tile = lax.axis_index("img"), lax.axis_index("tile")
    z, core, x, y = img // 2, img % 2, tile // SIDE, tile % SIDE

    def at(dx, dy, dz, dc):
        return (
            lax.rem(z + dz + SIDE, SIDE) * 2 + lax.rem(core + dc, 2),
            lax.rem(x + dx + SIDE, SIDE) * SIDE + lax.rem(y + dy + SIDE, SIDE),
        )

    loads = [[], []]
    loads[0].append(pltpu.make_async_copy(counts, count_s, load_sem.at[0]))
    loads[0].append(pltpu.make_async_copy(centroids, centroid_v, load_sem.at[1]))
    for k in range(2):
        for n, (source, target) in enumerate(((ids, id_v), (weights, weight_v), (features, feature_v))):
            loads[k].append(pltpu.make_async_copy(source.at[k], target.at[k], load_sem.at[2 + 3 * k + n]))
    for copy in loads[0] + loads[1]:
        copy.start()

    distances = (2, 1, -1, 0)
    plane = [(dx, dy, 0, 0) for dx in distances for dy in distances if dx or dy]
    column = [(0, 0, dz, dc) for dz in distances for dc in (1, 0) if dz or dc]
    barrier = pltpu.get_barrier_semaphore()
    for step in plane + column:
        pl.semaphore_signal(barrier, inc=1, device_id=at(*step), device_id_type=MESH)
    fill = pltpu.make_async_copy(covariance, total, cov_sem.at[0])
    fill.start()

    def aggregate(k):
        for copy in loads[k]:
            copy.wait()
        slots = id_v.shape[2]
        labels = lax.broadcasted_iota(jnp.int32, (CLUSTERS, 1), 0)
        in_range = lax.broadcasted_iota(jnp.int32, (1, slots), 1) < count_s[k]
        assign = jnp.zeros((CLUSTERS, slots), jnp.float32)
        for slot in range(TOPK):
            weight = jnp.where(in_range, weight_v[k, slot : slot + 1, :].astype(jnp.float32), 0.0)
            assign = assign + jnp.where(id_v[k, slot : slot + 1, :] == labels, weight, 0.0)
        assign = assign.astype(jnp.bfloat16)
        weight_sum = jnp.sum(assign.astype(jnp.float32), axis=1, keepdims=True)
        residual = jnp.dot(assign, feature_v[k], preferred_element_type=jnp.float32)
        residual = residual - weight_sum * centroid_v[...].astype(jnp.float32)
        magnitude = jnp.sqrt(jnp.sum(residual * residual, axis=1, keepdims=True) + 1e-06)
        residual = residual / magnitude
        for half in range(2):
            lanes = slice(half * LANES, (half + 1) * LANES)
            for block in range(CLUSTERS // ROWS):
                vlad[k, block, half] = residual[block * ROWS : (block + 1) * ROWS, lanes]
            for block in range(CLUSTERS // COLS):
                cols[block, k, half * COLS : (half + 1) * COLS] = residual[block * COLS : (block + 1) * COLS, lanes]

    def put(source, target, send_sem, recv_sem, step):
        copy = pltpu.make_async_remote_copy(
            src_ref=source, dst_ref=target, send_sem=send_sem, recv_sem=recv_sem,
            device_id=at(*step), device_id_type=MESH,
        )
        copy.start()
        return copy

    def wait(ref, sem):
        pltpu.make_async_copy(ref, ref, sem).wait()

    def along(k, u, v):
        return (u, v, 0, 0) if k == 0 else (v, u, 0, 0)

    def column_pieces(k):
        pltpu.make_async_copy(cols.at[tile, k], right.at[0, 0, 0, k, 0], c_recv.at[0]).start()
        for step in plane:
            u, v = step[:2] if k == 0 else (step[1], step[0])
            target = right.at[0, 0, PLACE[BACK[v]], k, PLACE[BACK[u]]]
            put(cols.at[at(*step)[1], k], target, c_send.at[0], c_recv.at[0], step)

    def row_pieces(k):
        pltpu.make_async_copy(vlad.at[k, img], left.at[0, 0, 0, k, 0], z_recv.at[k, 0]).start()
        for step in column:
            n = PLACE[BACK[step[2]]]
            put(vlad.at[k, at(*step)[0]], left.at[0, n, step[3], k, 0], z_send.at[k], z_recv.at[k, n], step)

    def go_u(k, j):
        wait(left.at[0, j, :, k, 0], z_recv.at[k, j])
        for u in (2, 1, -1):
            target = left.at[0, j, :, k, PLACE[BACK[u]]]
            put(left.at[0, j, :, k, 0], target, u_send.at[k], u_recv.at[k, j], along(k, u, 0))

    onward = {}

    def go_v(k, j):
        wait(left.at[0, j, :, k, pl.ds(1, 3)], u_recv.at[k, j])
        for n, turn in enumerate((1, -1)):
            target = left.at[PLACE[-turn], j, :, k]
            onward[k, j, n] = put(
                left.at[0, j, :, k], target, v_send.at[k], v_recv.at[k, j, n], along(k, 0, turn)
            )

    def relay(k, j):
        for n, turn in enumerate((1, -1)):
            onward[k, j, n].wait_recv()
            source = left.at[PLACE[-turn], j, :, k, pl.ds(2 * n, 2)]
            target = left.at[PLACE[2], j, :, k, pl.ds(2 * n, 2)]
            put(source, target, r_send.at[k], r_recv.at[k], along(k, 0, turn))

    def twin(dz):
        n = PLACE[dz]
        return put(right.at[n, 0], right.at[n, 1], s_send.at[n + 4], s_recv.at[n + 4], (0, 0, 0, 1))

    flat_right = right.reshape(-1, LANES)
    flat_left = left.reshape(-1, LANES)

    def stack_rows(v):
        for k in range(ROWS):
            values = [flat_left[pl.ds(v * 1024 + half * ROWS + k, 64, stride=16), :] for half in range(2)]
            top, rest = split(jnp.concatenate(values, axis=1))
            stacked[k, v * 64 : (v + 1) * 64] = top
            stacked[k, 192 + v * 64 : 192 + (v + 1) * 64] = rest
            if v < 2:
                stacked[k, 384 + v * 64 : 384 + (v + 1) * 64] = top
            else:
                spare_rows[k] = top

    def stack_columns(j):
        for v in range(SIDE - 1):
            blocks = []
            for k in range(COLS):
                for half in range(2):
                    start = (2 * j * SIDE + v) * 64 + half * COLS + k
                    pieces = [flat_right[pl.ds(start + core * 256, 8, stride=8), :] for core in range(2)]
                    blocks.append(jnp.concatenate(pieces, axis=0))
            top, rest = split(jnp.concatenate(blocks, axis=1))
            start = v * 64 + j * 16
            factor[start : start + 16] = top
            factor[192 + start : 192 + start + 16] = top
            if v < 2:
                factor[384 + start : 384 + start + 16] = rest
            else:
                spare_columns[j * 16 : (j + 1) * 16] = rest

    aggregate(0)
    pl.semaphore_wait(barrier, len(plane + column))
    column_pieces(0)
    row_pieces(0)
    aggregate(1)
    column_pieces(1)
    row_pieces(1)
    for k in range(2):
        go_u(k, 0)
    for k in range(2):
        go_u(k, 1)
    for k in range(2):
        go_u(k, 2)
    for k in range(2):
        go_u(k, 3)
    wait(right.at[0, 0], c_recv.at[0])
    spread = {
        dz: put(
            right.at[0, 0], right.at[PLACE[BACK[dz]], 0], s_send.at[PLACE[dz]], s_recv.at[PLACE[dz]],
            (0, 0, dz, 0),
        )
        for dz in (2, 1, -1)
    }
    twins = [twin(0)]
    for k in range(2):
        go_v(k, 0)
    for k in range(2):
        go_v(k, 1)
    for k in range(2):
        go_v(k, 2)
    for k in range(2):
        go_v(k, 3)
    stack_rows(0)
    for dz in (1, -1):
        spread[dz].wait_recv()
        twins.append(twin(BACK[dz]))
    for k in range(2):
        relay(k, 0)
    for k in range(2):
        relay(k, 1)
    spread[2].wait_recv()
    twins.append(twin(2))
    for k in range(2):
        relay(k, 2)
    for k in range(2):
        relay(k, 3)
    twins[0].wait_recv()
    stack_columns(0)
    twins[1].wait_recv()
    stack_columns(1)
    twins[2].wait_recv()
    stack_columns(2)
    stack_rows(1)
    stack_rows(2)
    twins[3].wait_recv()
    stack_columns(3)
    fill.wait()
    for k in range(ROWS):
        total[k * DESC : (k + 1) * DESC] += lax.dot_general(
            stacked[k], factor[...], DIMS, preferred_element_type=jnp.float32
        )

    wait(cols.at[pl.ds(0, 15)], c_send.at[0])
    for copy in list(spread.values()) + twins:
        copy.wait_send()
    for k in range(2):
        wait(vlad.at[k, pl.ds(0, 7)], z_send.at[k])
        wait(left.at[0, :, :, k, pl.ds(1, 3)], u_send.at[k])
        wait(left.at[pl.ds(1, 2), :, :, k], v_send.at[k])
        wait(left.at[3, :, :, k], r_send.at[k])
        wait(left.at[3, :, :, k], r_recv.at[k])


def product_kernel(left, right, total, spare_rows, spare_columns, updated, staged, factor, sems):
    top, rest = columns_of(right, SIDE - 1)
    factor[:64] = top
    factor[64:128] = top
    factor[128:192] = rest
    factor[192:] = spare_columns[...]
    copies = []
    for k in range(ROWS):
        rows = slice(k * DESC, (k + 1) * DESC)
        staged[rows] = total[rows] + lax.dot_general(
            jnp.concatenate([rows_of(left, 192, 64, k), spare_rows[k]], axis=0),
            factor[...],
            DIMS,
            preferred_element_type=jnp.float32,
        )
        copies.append(pltpu.make_async_copy(staged.at[rows], updated.at[rows], sems.at[k]))
        copies[-1].start()
    for copy in copies:
        copy.wait()


def body(features, cluster_ids, soft_weights, counts, centroids, covariance):
    images = features.shape[0]
    height, width = covariance.shape
    vmem = pl.BlockSpec(memory_space=pltpu.VMEM)
    hbm = pl.BlockSpec(memory_space=pltpu.HBM)
    dma = pltpu.SemaphoreType.DMA
    operands = (counts, features, cluster_ids, soft_weights, centroids, covariance)
    left, right, *rest = pl.pallas_call(
        gather_kernel,
        in_specs=[hbm] * 6,
        out_specs=[vmem] * 5,
        out_shape=[
            jax.ShapeDtypeStruct((SIDE, SIDE, 2, images, SIDE, 2, ROWS, LANES), jnp.float32),
            jax.ShapeDtypeStruct((SIDE, 2, SIDE, images, SIDE, 2 * COLS, LANES), jnp.float32),
            jax.ShapeDtypeStruct((height, width), jnp.float32),
            jax.ShapeDtypeStruct((ROWS, 64, DESC), jnp.bfloat16),
            jax.ShapeDtypeStruct((64, width), jnp.bfloat16),
        ],
        scratch_shapes=[
            pltpu.SMEM((images,), jnp.int32),
            pltpu.VMEM(features.shape, features.dtype),
            pltpu.VMEM(cluster_ids.shape, cluster_ids.dtype),
            pltpu.VMEM(soft_weights.shape, soft_weights.dtype),
            pltpu.VMEM(centroids.shape, centroids.dtype),
            pltpu.VMEM((images, CLUSTERS // ROWS, 2, ROWS, LANES), jnp.float32),
            pltpu.VMEM((16, images, 2 * COLS, LANES), jnp.float32),
            pltpu.VMEM((512, width), jnp.bfloat16),
            pltpu.VMEM((ROWS, 512, DESC), jnp.bfloat16),
            dma((8,)), dma((1,)), dma((2,)), dma((2, 4)), dma((2,)), dma((2, 4)),
            dma((2,)), dma((2, 4, 2)), dma((2,)), dma((2,)), dma((1,)), dma((1,)), dma((8,)), dma((8,)),
        ],
        compiler_params=pltpu.CompilerParams(
            collective_id=0, has_side_effects=True, vmem_limit_bytes=32 * 2**20
        ),
        name="gather",
    )(*(pltpu.with_memory_space_constraint(value, pltpu.HBM) for value in operands))
    return pl.pallas_call(
        product_kernel,
        in_specs=[vmem] * 5,
        out_specs=hbm,
        out_shape=jax.ShapeDtypeStruct((height, width), jnp.float32),
        scratch_shapes=[
            pltpu.VMEM((height, width), jnp.float32),
            pltpu.VMEM((256, width), jnp.bfloat16),
            dma((ROWS,)),
        ],
        compiler_params=pltpu.CompilerParams(vmem_limit_bytes=32 * 2**20),
        name="product",
    )(left.reshape(-1, LANES), right.reshape(-1, LANES), *rest)


def solution(mesh):
    return jax.shard_map(
        body,
        mesh=mesh,
        in_specs=(
            P(("img", "tile"), None, None),
            P(("img", "tile"), None, None),
            P(("img", "tile"), None, None),
            P(("img", "tile")),
            P(),
            P("img", "tile"),
        ),
        out_specs=P("img", "tile"),
        check_vma=False,
    )
```

```python
import jax
import jax.numpy as jnp
from jax import lax
from jax.experimental import pallas as pl
from jax.experimental.pallas import tpu as pltpu
from jax.sharding import PartitionSpec as P

MESH = pl.DeviceIdType.MESH
CLUSTERS, DESC, TOPK, IMAGES = 64, 256, 4, 256
SIDE = 4
ROWS = 8
COLS = 4
LANES = 128
PLACE = {0: 0, -1: 1, 1: 2, 2: 3}
BACK = {0: 0, -1: 1, 1: -1, 2: 2}
DIMS = (((0,), (0,)), ((), ()))


def split(value):
    top = value.astype(jnp.bfloat16)
    return top, (value - top.astype(jnp.float32)).astype(jnp.bfloat16)


def columns_of(right, v):
    blocks = []
    for j in range(COLS):
        halves = []
        for half in range(2):
            halves.append(
                jnp.concatenate(
                    [
                        right[pl.ds((zc * SIDE + v) * 64 + half * COLS + j, 8, stride=8), :]
                        for zc in range(8)
                    ],
                    axis=0,
                )
            )
        blocks.append(jnp.concatenate(halves, axis=1))
    top, rest = split(jnp.concatenate(blocks, axis=1))
    return top, rest


def rows_of(left, start, count, k):
    top, rest = split(
        jnp.concatenate(
            [left[pl.ds(start * 16 + half * ROWS + k, count, stride=16), :] for half in range(2)], axis=1
        )
    )
    return jnp.concatenate([top, rest, top], axis=0)


def gather_kernel(
    counts, features, ids, weights, centroids, covariance,
    left, right, total, spare_rows, spare_columns,
    count_s, feature_v, id_v, weight_v, centroid_v, vlad, cols, factor, stacked,
    load_sem, cov_sem, z_send, z_recv, u_send, u_recv, v_send, v_recv, r_send, r_recv,
    c_send, c_recv, s_send, s_recv,
):
    img, tile = lax.axis_index("img"), lax.axis_index("tile")
    z, core, x, y = img // 2, img % 2, tile // SIDE, tile % SIDE

    def at(dx, dy, dz, dc):
        return (
            lax.rem(z + dz + SIDE, SIDE) * 2 + lax.rem(core + dc, 2),
            lax.rem(x + dx + SIDE, SIDE) * SIDE + lax.rem(y + dy + SIDE, SIDE),
        )

    loads = [[], []]
    loads[0].append(pltpu.make_async_copy(counts, count_s, load_sem.at[0]))
    loads[0].append(pltpu.make_async_copy(centroids, centroid_v, load_sem.at[1]))
    for k in range(2):
        for n, (source, target) in enumerate(((ids, id_v), (weights, weight_v), (features, feature_v))):
            loads[k].append(pltpu.make_async_copy(source.at[k], target.at[k], load_sem.at[2 + 3 * k + n]))
    for copy in loads[0] + loads[1]:
        copy.start()

    distances = (2, 1, -1, 0)
    plane = [(dx, dy, 0, 0) for dx in distances for dy in distances if dx or dy]
    column = [(0, 0, dz, dc) for dz in distances for dc in (1, 0) if dz or dc]
    barrier = pltpu.get_barrier_semaphore()
    for step in plane + column:
        pl.semaphore_signal(barrier, inc=1, device_id=at(*step), device_id_type=MESH)
    fill = pltpu.make_async_copy(covariance, total, cov_sem.at[0])
    fill.start()

    def aggregate(k):
        for copy in loads[k]:
            copy.wait()
        slots = id_v.shape[2]
        labels = lax.broadcasted_iota(jnp.int32, (CLUSTERS, 1), 0)
        in_range = lax.broadcasted_iota(jnp.int32, (1, slots), 1) < count_s[k]
        assign = jnp.zeros((CLUSTERS, slots), jnp.float32)
        for slot in range(TOPK):
            weight = jnp.where(in_range, weight_v[k, slot : slot + 1, :].astype(jnp.float32), 0.0)
            assign = assign + jnp.where(id_v[k, slot : slot + 1, :] == labels, weight, 0.0)
        assign = assign.astype(jnp.bfloat16)
        weight_sum = jnp.sum(assign.astype(jnp.float32), axis=1, keepdims=True)
        residual = jnp.dot(assign, feature_v[k], preferred_element_type=jnp.float32)
        residual = residual - weight_sum * centroid_v[...].astype(jnp.float32)
        magnitude = jnp.sqrt(jnp.sum(residual * residual, axis=1, keepdims=True) + 1e-06)
        residual = residual / magnitude
        for half in range(2):
            lanes = slice(half * LANES, (half + 1) * LANES)
            for block in range(CLUSTERS // ROWS):
                vlad[k, block, half] = residual[block * ROWS : (block + 1) * ROWS, lanes]
            for block in range(CLUSTERS // COLS):
                cols[block, k, half * COLS : (half + 1) * COLS] = residual[block * COLS : (block + 1) * COLS, lanes]

    def put(source, target, send_sem, recv_sem, step):
        copy = pltpu.make_async_remote_copy(
            src_ref=source, dst_ref=target, send_sem=send_sem, recv_sem=recv_sem,
            device_id=at(*step), device_id_type=MESH,
        )
        copy.start()
        return copy

    def wait(ref, sem):
        pltpu.make_async_copy(ref, ref, sem).wait()

    def along(k, u, v):
        return (u, v, 0, 0) if k == 0 else (v, u, 0, 0)

    def column_pieces(k):
        pltpu.make_async_copy(cols.at[tile, k], right.at[0, 0, 0, k, 0], c_recv.at[0]).start()
        for step in plane:
            u, v = step[:2] if k == 0 else (step[1], step[0])
            target = right.at[0, 0, PLACE[BACK[v]], k, PLACE[BACK[u]]]
            put(cols.at[at(*step)[1], k], target, c_send.at[0], c_recv.at[0], step)

    def row_pieces(k):
        pltpu.make_async_copy(vlad.at[k, img], left.at[0, 0, 0, k, 0], z_recv.at[k, 0]).start()
        for step in column:
            n = PLACE[BACK[step[2]]]
            put(vlad.at[k, at(*step)[0]], left.at[0, n, step[3], k, 0], z_send.at[k], z_recv.at[k, n], step)

    def go_u(k, j):
        wait(left.at[0, j, :, k, 0], z_recv.at[k, j])
        for u in (2, 1, -1):
            target = left.at[0, j, :, k, PLACE[BACK[u]]]
            put(left.at[0, j, :, k, 0], target, u_send.at[k], u_recv.at[k, j], along(k, u, 0))

    def second(k, j, slots):
        for n, turn in enumerate((1, -1)):
            target = left.at[PLACE[-turn], j, :, k, slots]
            put(left.at[0, j, :, k, slots], target, v_send.at[k], v_recv.at[k, j, n], along(k, 0, turn))

    def go_own(k, j):
        second(k, j, pl.ds(0, 1))

    def go_v(k, j):
        wait(left.at[0, j, :, k, pl.ds(1, 3)], u_recv.at[k, j])
        second(k, j, pl.ds(1, 3))

    def relay(k, j):
        for n, turn in enumerate((1, -1)):
            wait(left.at[PLACE[-turn], j, :, k], v_recv.at[k, j, n])
            source = left.at[PLACE[-turn], j, :, k, pl.ds(2 * n, 2)]
            target = left.at[PLACE[2], j, :, k, pl.ds(2 * n, 2)]
            put(source, target, r_send.at[k], r_recv.at[k], along(k, 0, turn))

    def twin(dz):
        n = PLACE[dz]
        return put(right.at[n, 0], right.at[n, 1], s_send.at[n + 4], s_recv.at[n + 4], (0, 0, 0, 1))

    flat_right = right.reshape(-1, LANES)
    flat_left = left.reshape(-1, LANES)

    def stack_rows(v):
        for k in range(ROWS):
            values = [flat_left[pl.ds(v * 1024 + half * ROWS + k, 64, stride=16), :] for half in range(2)]
            top, rest = split(jnp.concatenate(values, axis=1))
            stacked[k, v * 64 : (v + 1) * 64] = top
            stacked[k, 192 + v * 64 : 192 + (v + 1) * 64] = rest
            if v < 2:
                stacked[k, 384 + v * 64 : 384 + (v + 1) * 64] = top
            else:
                spare_rows[k] = top

    def stack_columns(j):
        for v in range(SIDE - 1):
            blocks = []
            for k in range(COLS):
                for half in range(2):
                    start = (2 * j * SIDE + v) * 64 + half * COLS + k
                    pieces = [flat_right[pl.ds(start + core * 256, 8, stride=8), :] for core in range(2)]
                    blocks.append(jnp.concatenate(pieces, axis=0))
            top, rest = split(jnp.concatenate(blocks, axis=1))
            start = v * 64 + j * 16
            factor[start : start + 16] = top
            factor[192 + start : 192 + start + 16] = top
            if v < 2:
                factor[384 + start : 384 + start + 16] = rest
            else:
                spare_columns[j * 16 : (j + 1) * 16] = rest

    aggregate(0)
    pl.semaphore_wait(barrier, len(plane + column))
    row_pieces(0)
    column_pieces(0)
    aggregate(1)
    row_pieces(1)
    column_pieces(1)
    for k in range(2):
        go_u(k, 0)
    for k in range(2):
        go_u(k, 1)
    for k in range(2):
        go_u(k, 2)
    for k in range(2):
        go_u(k, 3)
    for k in range(2):
        go_own(k, 0)
    for k in range(2):
        go_own(k, 1)
    for k in range(2):
        go_own(k, 2)
    for k in range(2):
        go_own(k, 3)
    wait(right.at[0, 0], c_recv.at[0])
    spread = {
        dz: put(
            right.at[0, 0], right.at[PLACE[BACK[dz]], 0], s_send.at[PLACE[dz]], s_recv.at[PLACE[dz]],
            (0, 0, dz, 0),
        )
        for dz in (2, 1, -1)
    }
    twins = [twin(0)]
    for k in range(2):
        go_v(k, 0)
    for k in range(2):
        go_v(k, 1)
    for k in range(2):
        go_v(k, 2)
    for k in range(2):
        go_v(k, 3)
    stack_rows(0)
    for dz in (1, -1):
        spread[dz].wait_recv()
        twins.append(twin(BACK[dz]))
    for k in range(2):
        relay(k, 0)
    for k in range(2):
        relay(k, 1)
    spread[2].wait_recv()
    twins.append(twin(2))
    for k in range(2):
        relay(k, 2)
    for k in range(2):
        relay(k, 3)
    twins[0].wait_recv()
    stack_columns(0)
    twins[1].wait_recv()
    stack_columns(1)
    twins[2].wait_recv()
    stack_columns(2)
    stack_rows(1)
    stack_rows(2)
    twins[3].wait_recv()
    stack_columns(3)
    fill.wait()
    for k in range(ROWS):
        total[k * DESC : (k + 1) * DESC] += lax.dot_general(
            stacked[k], factor[...], DIMS, preferred_element_type=jnp.float32
        )

    wait(cols.at[pl.ds(0, 15)], c_send.at[0])
    for copy in list(spread.values()) + twins:
        copy.wait_send()
    for k in range(2):
        wait(vlad.at[k, pl.ds(0, 7)], z_send.at[k])
        wait(left.at[0, :, :, k, pl.ds(1, 3)], u_send.at[k])
        wait(left.at[pl.ds(1, 2), :, :, k], v_send.at[k])
        wait(left.at[3, :, :, k], r_send.at[k])
        wait(left.at[3, :, :, k], r_recv.at[k])


def product_kernel(left, right, total, spare_rows, spare_columns, updated, staged, factor, sems):
    top, rest = columns_of(right, SIDE - 1)
    factor[:64] = top
    factor[64:128] = top
    factor[128:192] = rest
    factor[192:] = spare_columns[...]
    copies = []
    for k in range(ROWS):
        rows = slice(k * DESC, (k + 1) * DESC)
        staged[rows] = total[rows] + lax.dot_general(
            jnp.concatenate([rows_of(left, 192, 64, k), spare_rows[k]], axis=0),
            factor[...],
            DIMS,
            preferred_element_type=jnp.float32,
        )
        copies.append(pltpu.make_async_copy(staged.at[rows], updated.at[rows], sems.at[k]))
        copies[-1].start()
    for copy in copies:
        copy.wait()


def body(features, cluster_ids, soft_weights, counts, centroids, covariance):
    images = features.shape[0]
    height, width = covariance.shape
    vmem = pl.BlockSpec(memory_space=pltpu.VMEM)
    hbm = pl.BlockSpec(memory_space=pltpu.HBM)
    dma = pltpu.SemaphoreType.DMA
    operands = (counts, features, cluster_ids, soft_weights, centroids, covariance)
    left, right, *rest = pl.pallas_call(
        gather_kernel,
        in_specs=[hbm] * 6,
        out_specs=[vmem] * 5,
        out_shape=[
            jax.ShapeDtypeStruct((SIDE, SIDE, 2, images, SIDE, 2, ROWS, LANES), jnp.float32),
            jax.ShapeDtypeStruct((SIDE, 2, SIDE, images, SIDE, 2 * COLS, LANES), jnp.float32),
            jax.ShapeDtypeStruct((height, width), jnp.float32),
            jax.ShapeDtypeStruct((ROWS, 64, DESC), jnp.bfloat16),
            jax.ShapeDtypeStruct((64, width), jnp.bfloat16),
        ],
        scratch_shapes=[
            pltpu.SMEM((images,), jnp.int32),
            pltpu.VMEM(features.shape, features.dtype),
            pltpu.VMEM(cluster_ids.shape, cluster_ids.dtype),
            pltpu.VMEM(soft_weights.shape, soft_weights.dtype),
            pltpu.VMEM(centroids.shape, centroids.dtype),
            pltpu.VMEM((images, CLUSTERS // ROWS, 2, ROWS, LANES), jnp.float32),
            pltpu.VMEM((16, images, 2 * COLS, LANES), jnp.float32),
            pltpu.VMEM((512, width), jnp.bfloat16),
            pltpu.VMEM((ROWS, 512, DESC), jnp.bfloat16),
            dma((8,)), dma((1,)), dma((2,)), dma((2, 4)), dma((2,)), dma((2, 4)),
            dma((2,)), dma((2, 4, 2)), dma((2,)), dma((2,)), dma((1,)), dma((1,)), dma((8,)), dma((8,)),
        ],
        compiler_params=pltpu.CompilerParams(
            collective_id=0, has_side_effects=True, vmem_limit_bytes=32 * 2**20
        ),
        name="gather",
    )(*(pltpu.with_memory_space_constraint(value, pltpu.HBM) for value in operands))
    return pl.pallas_call(
        product_kernel,
        in_specs=[vmem] * 5,
        out_specs=hbm,
        out_shape=jax.ShapeDtypeStruct((height, width), jnp.float32),
        scratch_shapes=[
            pltpu.VMEM((height, width), jnp.float32),
            pltpu.VMEM((256, width), jnp.bfloat16),
            dma((ROWS,)),
        ],
        compiler_params=pltpu.CompilerParams(vmem_limit_bytes=32 * 2**20),
        name="product",
    )(left.reshape(-1, LANES), right.reshape(-1, LANES), *rest)


def solution(mesh):
    return jax.shard_map(
        body,
        mesh=mesh,
        in_specs=(
            P(("img", "tile"), None, None),
            P(("img", "tile"), None, None),
            P(("img", "tile"), None, None),
            P(("img", "tile")),
            P(),
            P("img", "tile"),
        ),
        out_specs=P("img", "tile"),
        check_vma=False,
    )
```

```python
import jax
import jax.numpy as jnp
from jax import lax
from jax.experimental import pallas as pl
from jax.experimental.pallas import tpu as pltpu
from jax.sharding import PartitionSpec as P

MESH = pl.DeviceIdType.MESH
CLUSTERS, DESC, TOPK, IMAGES = 64, 256, 4, 256
SIDE = 4
ROWS = 8
COLS = 4
LANES = 128
PLACE = {0: 0, -1: 1, 1: 2, 2: 3}
BACK = {0: 0, -1: 1, 1: -1, 2: 2}
DIMS = (((0,), (0,)), ((), ()))


def split(value):
    top = value.astype(jnp.bfloat16)
    return top, (value - top.astype(jnp.float32)).astype(jnp.bfloat16)


def columns_of(right, v):
    blocks = []
    for j in range(COLS):
        halves = []
        for half in range(2):
            halves.append(
                jnp.concatenate(
                    [
                        right[pl.ds((zc * SIDE + v) * 64 + half * COLS + j, 8, stride=8), :]
                        for zc in range(8)
                    ],
                    axis=0,
                )
            )
        blocks.append(jnp.concatenate(halves, axis=1))
    top, rest = split(jnp.concatenate(blocks, axis=1))
    return top, rest


def rows_of(left, start, count, k):
    top, rest = split(
        jnp.concatenate(
            [left[pl.ds(start * 16 + half * ROWS + k, count, stride=16), :] for half in range(2)], axis=1
        )
    )
    return jnp.concatenate([top, rest, top], axis=0)


def gather_kernel(
    counts, features, ids, weights, centroids, covariance,
    left, right, total, spare_rows, spare_columns,
    count_s, feature_v, id_v, weight_v, centroid_v, vlad, cols, factor, stacked,
    load_sem, cov_sem, z_send, z_recv, u_send, u_recv, v_send, v_recv, r_send, r_recv,
    c_send, c_recv, s_send, s_recv,
):
    img, tile = lax.axis_index("img"), lax.axis_index("tile")
    z, core, x, y = img // 2, img % 2, tile // SIDE, tile % SIDE

    def at(dx, dy, dz, dc):
        return (
            lax.rem(z + dz + SIDE, SIDE) * 2 + lax.rem(core + dc, 2),
            lax.rem(x + dx + SIDE, SIDE) * SIDE + lax.rem(y + dy + SIDE, SIDE),
        )

    loads = [[], []]
    loads[0].append(pltpu.make_async_copy(counts, count_s, load_sem.at[0]))
    loads[0].append(pltpu.make_async_copy(centroids, centroid_v, load_sem.at[1]))
    for k in range(2):
        for n, (source, target) in enumerate(((ids, id_v), (weights, weight_v), (features, feature_v))):
            loads[k].append(pltpu.make_async_copy(source.at[k], target.at[k], load_sem.at[2 + 3 * k + n]))
    for copy in loads[0] + loads[1]:
        copy.start()

    distances = (2, 1, -1, 0)
    plane = [(dx, dy, 0, 0) for dx in distances for dy in distances if dx or dy]
    column = [(0, 0, dz, dc) for dz in distances for dc in (1, 0) if dz or dc]
    barrier = pltpu.get_barrier_semaphore()
    for step in plane + column:
        pl.semaphore_signal(barrier, inc=1, device_id=at(*step), device_id_type=MESH)
    fill = pltpu.make_async_copy(covariance, total, cov_sem.at[0])
    fill.start()

    def aggregate(k):
        for copy in loads[k]:
            copy.wait()
        slots = id_v.shape[2]
        labels = lax.broadcasted_iota(jnp.int32, (CLUSTERS, 1), 0)
        in_range = lax.broadcasted_iota(jnp.int32, (1, slots), 1) < count_s[k]
        assign = jnp.zeros((CLUSTERS, slots), jnp.float32)
        for slot in range(TOPK):
            weight = jnp.where(in_range, weight_v[k, slot : slot + 1, :].astype(jnp.float32), 0.0)
            assign = assign + jnp.where(id_v[k, slot : slot + 1, :] == labels, weight, 0.0)
        assign = assign.astype(jnp.bfloat16)
        weight_sum = jnp.sum(assign.astype(jnp.float32), axis=1, keepdims=True)
        residual = jnp.dot(assign, feature_v[k], preferred_element_type=jnp.float32)
        residual = residual - weight_sum * centroid_v[...].astype(jnp.float32)
        magnitude = jnp.sqrt(jnp.sum(residual * residual, axis=1, keepdims=True) + 1e-06)
        residual = residual / magnitude
        for half in range(2):
            lanes = slice(half * LANES, (half + 1) * LANES)
            for block in range(CLUSTERS // ROWS):
                vlad[k, block, half] = residual[block * ROWS : (block + 1) * ROWS, lanes]
            for block in range(CLUSTERS // COLS):
                cols[block, k, half * COLS : (half + 1) * COLS] = residual[block * COLS : (block + 1) * COLS, lanes]

    def put(source, target, send_sem, recv_sem, step):
        copy = pltpu.make_async_remote_copy(
            src_ref=source, dst_ref=target, send_sem=send_sem, recv_sem=recv_sem,
            device_id=at(*step), device_id_type=MESH,
        )
        copy.start()
        return copy

    def wait(ref, sem):
        pltpu.make_async_copy(ref, ref, sem).wait()

    def along(k, u, v):
        return (u, v, 0, 0) if k == 0 else (v, u, 0, 0)

    def column_pieces(k):
        pltpu.make_async_copy(cols.at[tile, k], right.at[0, 0, 0, k, 0], c_recv.at[0]).start()
        for step in plane:
            u, v = step[:2] if k == 0 else (step[1], step[0])
            target = right.at[0, 0, PLACE[BACK[v]], k, PLACE[BACK[u]]]
            put(cols.at[at(*step)[1], k], target, c_send.at[0], c_recv.at[0], step)

    def row_pieces(k):
        pltpu.make_async_copy(vlad.at[k, img], left.at[0, 0, 0, k, 0], z_recv.at[k, 0]).start()
        for step in column:
            n = PLACE[BACK[step[2]]]
            put(vlad.at[k, at(*step)[0]], left.at[0, n, step[3], k, 0], z_send.at[k], z_recv.at[k, n], step)

    def go_u(k, j):
        wait(left.at[0, j, :, k, 0], z_recv.at[k, j])
        for u in (2, 1, -1):
            target = left.at[0, j, :, k, PLACE[BACK[u]]]
            put(left.at[0, j, :, k, 0], target, u_send.at[k], u_recv.at[k, j], along(k, u, 0))

    def second(k, j, slots):
        for n, turn in enumerate((1, -1)):
            target = left.at[PLACE[-turn], j, :, k, slots]
            put(left.at[0, j, :, k, slots], target, v_send.at[k], v_recv.at[k, j, n], along(k, 0, turn))

    def go_own(k, j):
        second(k, j, pl.ds(0, 1))

    def go_v(k, j):
        wait(left.at[0, j, :, k, pl.ds(1, 3)], u_recv.at[k, j])
        second(k, j, pl.ds(1, 3))

    def relay(k, j):
        for n, turn in enumerate((1, -1)):
            wait(left.at[PLACE[-turn], j, :, k], v_recv.at[k, j, n])
            source = left.at[PLACE[-turn], j, :, k, pl.ds(2 * n, 2)]
            target = left.at[PLACE[2], j, :, k, pl.ds(2 * n, 2)]
            put(source, target, r_send.at[k], r_recv.at[k], along(k, 0, turn))

    def twin(dz):
        n = PLACE[dz]
        return put(right.at[n, 0], right.at[n, 1], s_send.at[n + 4], s_recv.at[n + 4], (0, 0, 0, 1))

    flat_right = right.reshape(-1, LANES)
    flat_left = left.reshape(-1, LANES)

    def stack_rows(v, clusters=range(ROWS)):
        for k in clusters:
            values = [flat_left[pl.ds(v * 1024 + half * ROWS + k, 64, stride=16), :] for half in range(2)]
            top, rest = split(jnp.concatenate(values, axis=1))
            stacked[k, v * 64 : (v + 1) * 64] = top
            stacked[k, 192 + v * 64 : 192 + (v + 1) * 64] = rest
            if v < 2:
                stacked[k, 384 + v * 64 : 384 + (v + 1) * 64] = top
            else:
                spare_rows[k] = top

    def stack_columns(j):
        for v in range(SIDE - 1):
            blocks = []
            for k in range(COLS):
                for half in range(2):
                    start = (2 * j * SIDE + v) * 64 + half * COLS + k
                    pieces = [flat_right[pl.ds(start + core * 256, 8, stride=8), :] for core in range(2)]
                    blocks.append(jnp.concatenate(pieces, axis=0))
            top, rest = split(jnp.concatenate(blocks, axis=1))
            start = v * 64 + j * 16
            factor[start : start + 16] = top
            factor[192 + start : 192 + start + 16] = top
            if v < 2:
                factor[384 + start : 384 + start + 16] = rest
            else:
                spare_columns[j * 16 : (j + 1) * 16] = rest

    aggregate(0)
    pl.semaphore_wait(barrier, len(plane + column))
    row_pieces(0)
    column_pieces(0)
    aggregate(1)
    row_pieces(1)
    column_pieces(1)
    for k in range(2):
        go_u(k, 0)
    for k in range(2):
        go_u(k, 1)
    for k in range(2):
        go_u(k, 2)
    for k in range(2):
        go_u(k, 3)
    for k in range(2):
        go_own(k, 0)
    for k in range(2):
        go_own(k, 1)
    for k in range(2):
        go_own(k, 2)
    for k in range(2):
        go_own(k, 3)
    wait(right.at[0, 0], c_recv.at[0])
    spread = {
        dz: put(
            right.at[0, 0], right.at[PLACE[BACK[dz]], 0], s_send.at[PLACE[dz]], s_recv.at[PLACE[dz]],
            (0, 0, dz, 0),
        )
        for dz in (2, 1, -1)
    }
    twins = [twin(0)]
    for k in range(2):
        go_v(k, 0)
    for k in range(2):
        go_v(k, 1)
    for k in range(2):
        go_v(k, 2)
    for k in range(2):
        go_v(k, 3)
    stack_rows(0)
    for dz in (1, -1):
        spread[dz].wait_recv()
        twins.append(twin(BACK[dz]))
    for k in range(2):
        relay(k, 0)
    for k in range(2):
        relay(k, 1)
    spread[2].wait_recv()
    twins.append(twin(2))
    for k in range(2):
        relay(k, 2)
    for k in range(2):
        relay(k, 3)
    twins[0].wait_recv()
    stack_columns(0)
    twins[1].wait_recv()
    stack_columns(1)
    twins[2].wait_recv()
    stack_columns(2)
    twins[3].wait_recv()
    stack_columns(3)
    fill.wait()
    for k in range(ROWS):
        stack_rows(1, (k,))
        stack_rows(2, (k,))
        total[k * DESC : (k + 1) * DESC] += lax.dot_general(
            stacked[k], factor[...], DIMS, preferred_element_type=jnp.float32
        )

    wait(cols.at[pl.ds(0, 15)], c_send.at[0])
    for copy in list(spread.values()) + twins:
        copy.wait_send()
    for k in range(2):
        wait(vlad.at[k, pl.ds(0, 7)], z_send.at[k])
        wait(left.at[0, :, :, k, pl.ds(1, 3)], u_send.at[k])
        wait(left.at[pl.ds(1, 2), :, :, k], v_send.at[k])
        wait(left.at[3, :, :, k], r_send.at[k])
        wait(left.at[3, :, :, k], r_recv.at[k])


def product_kernel(left, right, total, spare_rows, spare_columns, updated, staged, factor, sems):
    top, rest = columns_of(right, SIDE - 1)
    factor[:64] = top
    factor[64:128] = top
    factor[128:192] = rest
    factor[192:] = spare_columns[...]
    copies = []
    for k in range(ROWS):
        rows = slice(k * DESC, (k + 1) * DESC)
        staged[rows] = total[rows] + lax.dot_general(
            jnp.concatenate([rows_of(left, 192, 64, k), spare_rows[k]], axis=0),
            factor[...],
            DIMS,
            preferred_element_type=jnp.float32,
        )
        copies.append(pltpu.make_async_copy(staged.at[rows], updated.at[rows], sems.at[k]))
        copies[-1].start()
    for copy in copies:
        copy.wait()


def body(features, cluster_ids, soft_weights, counts, centroids, covariance):
    images = features.shape[0]
    height, width = covariance.shape
    vmem = pl.BlockSpec(memory_space=pltpu.VMEM)
    hbm = pl.BlockSpec(memory_space=pltpu.HBM)
    dma = pltpu.SemaphoreType.DMA
    operands = (counts, features, cluster_ids, soft_weights, centroids, covariance)
    left, right, *rest = pl.pallas_call(
        gather_kernel,
        in_specs=[hbm] * 6,
        out_specs=[vmem] * 5,
        out_shape=[
            jax.ShapeDtypeStruct((SIDE, SIDE, 2, images, SIDE, 2, ROWS, LANES), jnp.float32),
            jax.ShapeDtypeStruct((SIDE, 2, SIDE, images, SIDE, 2 * COLS, LANES), jnp.float32),
            jax.ShapeDtypeStruct((height, width), jnp.float32),
            jax.ShapeDtypeStruct((ROWS, 64, DESC), jnp.bfloat16),
            jax.ShapeDtypeStruct((64, width), jnp.bfloat16),
        ],
        scratch_shapes=[
            pltpu.SMEM((images,), jnp.int32),
            pltpu.VMEM(features.shape, features.dtype),
            pltpu.VMEM(cluster_ids.shape, cluster_ids.dtype),
            pltpu.VMEM(soft_weights.shape, soft_weights.dtype),
            pltpu.VMEM(centroids.shape, centroids.dtype),
            pltpu.VMEM((images, CLUSTERS // ROWS, 2, ROWS, LANES), jnp.float32),
            pltpu.VMEM((16, images, 2 * COLS, LANES), jnp.float32),
            pltpu.VMEM((512, width), jnp.bfloat16),
            pltpu.VMEM((ROWS, 512, DESC), jnp.bfloat16),
            dma((8,)), dma((1,)), dma((2,)), dma((2, 4)), dma((2,)), dma((2, 4)),
            dma((2,)), dma((2, 4, 2)), dma((2,)), dma((2,)), dma((1,)), dma((1,)), dma((8,)), dma((8,)),
        ],
        compiler_params=pltpu.CompilerParams(
            collective_id=0, has_side_effects=True, vmem_limit_bytes=32 * 2**20
        ),
        name="gather",
    )(*(pltpu.with_memory_space_constraint(value, pltpu.HBM) for value in operands))
    return pl.pallas_call(
        product_kernel,
        in_specs=[vmem] * 5,
        out_specs=hbm,
        out_shape=jax.ShapeDtypeStruct((height, width), jnp.float32),
        scratch_shapes=[
            pltpu.VMEM((height, width), jnp.float32),
            pltpu.VMEM((256, width), jnp.bfloat16),
            dma((ROWS,)),
        ],
        compiler_params=pltpu.CompilerParams(vmem_limit_bytes=32 * 2**20),
        name="product",
    )(left.reshape(-1, LANES), right.reshape(-1, LANES), *rest)


def solution(mesh):
    return jax.shard_map(
        body,
        mesh=mesh,
        in_specs=(
            P(("img", "tile"), None, None),
            P(("img", "tile"), None, None),
            P(("img", "tile"), None, None),
            P(("img", "tile")),
            P(),
            P("img", "tile"),
        ),
        out_specs=P("img", "tile"),
        check_vma=False,
    )
```
